512 devices in a mesh: dp: 16 (over z), expert: 32 (over y, x, core).
Axes of the slice: x: 4, y: 4, z: 16, core: 2. Of those that a mesh axis runs over, the one named last changes fastest.
Arguments:
- activations: bfloat16 [65536, 3584], P(('dp', 'expert')), may hold values from -6 to 6
- out_grad: bfloat16 [65536, 3584], P(('dp', 'expert')), may hold values from -0.09375 to 0.09375
- router_weight: bfloat16 [128, 3584], P('expert'), may hold values from -0.09375 to 0.09375
- expert_ids: int32 [65536, 2], P(('dp', 'expert')), may hold values from 0 to 127, all different within a row; in each aligned block of 128 rows (0 to 127, 128 to 255, ...) at most 2 rows name the same one
- saved_output: bfloat16 [16, 128, 64, 3584], P('dp', 'expert'), may hold values from -6 to 6
Outputs:
- input_grad: bfloat16 [65536, 3584], P(('dp', 'expert'))
- score_grad: float32 [65536, 2], P(('dp', 'expert'))
- router_grad: float32 [128, 3584], P('expert')
The draws below stay inside these ranges and needn't reach their ends.
Inputs may be any that keep to these rules, and one draw needn't show every extreme that they name: `expert_ids`: within the 128 rows of one device no expert is named more than 2 times; a row names distinct experts.
All inputs are finite; a program needn't handle non-finite values.
Results may differ from the reference program's by a relative error of at most 0.0049.
Values may be sent and summed in bfloat16 or wider, within the bound.
No kernel may reach another device: no remote copies, remote signals or barrier semaphores. Data moves between devices by JAX's collectives and lax.ppermute only.
A program may use at most 64 MiB of HBM per device.

```python
import math
import jax
import jax.numpy as jnp
import numpy as np
from jax import lax

D = 3584
TOPK = 2
TOK_DEV = 128
EXPERTS = 128
MOST = 2
SLOTS = 64
GROUPS = 16
TOKENS = 65536
N_EXPERT = 32


def steps_of(stream_key, dims, cuts, low, top_value):
    def one(dim, blocks):
        heights = jax.random.uniform(jax.random.fold_in(jax.random.fold_in(stream_key, 6), dim), (blocks,), jnp.float32, low / len(cuts), top_value / len(cuts))
        return jnp.repeat(jnp.exp(heights), dims[dim] // blocks).reshape((-1,) + (1,) * (len(dims) - dim - 1))

    loudness = one(*cuts[0])
    for cut in cuts[1:]:
        loudness = loudness * one(*cut)
    return loudness


def shared_out(key, own, number, rows, number_of, top, reach, skew):
    sequence = jax.random.permutation(key, number_of)
    heavy_load, usual = shares(number_of, rows * top, reach, skew, True), shares(number_of, rows * top, reach, skew, False)
    places = jnp.arange(number_of)

    def named(tallies, turn):
        used = int((tallies > 0).sum())
        fixed = max(1, used // 4)
        moved = fixed + (places - fixed + turn * (used - fixed)) % max(1, number_of - fixed)
        return jnp.zeros((number_of,), jnp.int32).at[sequence[jnp.where(places < fixed, places, moved)]].set(jnp.asarray(tallies, jnp.int32))

    tallies = jnp.where(number % 4 == 0, named(heavy_load, number // 4), named(usual, number - number // 4 - 1))
    mixed = jax.random.permutation(jax.random.fold_in(own, 3), number_of)
    source_of, receiver = mixed[0:number_of // 2 * 2:2], mixed[1:number_of // 2 * 2:2]
    slack = jnp.minimum(tallies[source_of] - 1, reach - tallies[receiver]) // 2
    slack = jnp.where((source_of == sequence[0]) | (receiver == sequence[0]) | (tallies[receiver] == 0), 0, jnp.maximum(slack, 0))
    moved = jax.random.randint(jax.random.fold_in(own, 4), (number_of // 2,), 0, 1 << 20) % (slack + 1)
    tallies = tallies.at[source_of].add(-moved).at[receiver].add(moved)
    items = jnp.searchsorted(jnp.cumsum(tallies), jnp.arange(rows * top), side="right").astype(jnp.int32)
    listing = items.reshape(top, rows).T
    listing = listing[jax.random.permutation(jax.random.fold_in(own, 1), rows)]
    turn = jax.random.randint(jax.random.fold_in(own, 2), (rows, 1), 0, top)
    return jnp.take_along_axis(listing, (jnp.arange(top)[None, :] + turn) % top, axis=1)


def shares(count, total, most, lean, full):
    weights = [(1 << 20) // math.isqrt(standing ** lean) + 1 for standing in range(1, count + 1)]
    largest = most if full else min(most, max(-(-total // count), total * weights[0] // sum(weights)))
    least = 1 if total - largest >= count - 1 else 0
    given, surplus = [largest] + [least] * (count - 1), total - largest - least * (count - 1)
    while surplus > 0:
        movable = [i for i in range(1, count) if given[i] < largest] or [i for i in range(1, count) if given[i] < most]
        whole, left = sum([weights[i] for i in movable]), surplus
        for i in movable:
            more = min(most - given[i], max(1, left * weights[i] // whole), surplus)
            given[i] = given[i] + more
            surplus = surplus - more
    return np.array(given)


def bell_draw(stream_key, dims, width, limit, shards=(), kind=jnp.bfloat16):
    array = width * jax.random.normal(stream_key, dims, jnp.float32)
    if shards:
        array = array * steps_of(stream_key, dims, shards, -0.22, 0.18)
    return jnp.clip(array, -limit, limit).astype(kind)


def setup_inputs(seed: int = 0) -> dict:
    keys = jax.random.split(jax.random.key(seed), 6)
    activations = bell_draw(keys[0], (TOKENS, D), 1.0, 6.0, ((0, 512),))
    out_grad = bell_draw(keys[1], (TOKENS, D), D ** -0.5, 0.09375, ((0, 512),))
    router_weight = bell_draw(keys[2], (EXPERTS, D), D ** -0.5, 0.09375, ((0, 32),))
    expert_ids_keys = jax.random.split(jax.random.fold_in(keys[3], 1), TOKENS // TOK_DEV)
    expert_ids_turns = jax.random.permutation(jax.random.fold_in(keys[3], 3), TOKENS // TOK_DEV)
    expert_ids = jax.vmap(lambda own, number: shared_out(jax.random.fold_in(keys[3], 2), own, number, TOK_DEV, EXPERTS, TOPK, MOST, 2))(expert_ids_keys, expert_ids_turns).reshape((TOKENS, TOPK))
    saved_output = bell_draw(keys[4], (GROUPS, EXPERTS, SLOTS, D), 1.0, 6.0, ((0, 16), (1, 32)))
    return dict(activations=activations, out_grad=out_grad, router_weight=router_weight, expert_ids=expert_ids, saved_output=saved_output)


route_scale = 2.5


def reference(activations, out_grad, router_weight, expert_ids, saved_output):
    expert_axis = jnp.arange(EXPERTS, dtype=jnp.int32)
    onehot = (expert_ids[:, :, None] == expert_axis[None, None, :]).astype(jnp.int32)
    per_token = jnp.sum(onehot, axis=1).reshape(TOKENS // TOK_DEV, TOK_DEV, EXPERTS)
    earlier = (jnp.cumsum(per_token, axis=1) - per_token).reshape(TOKENS, EXPERTS)
    slot_index = jnp.sum(onehot * earlier[:, None, :], axis=2).astype(jnp.int32)
    source = ((jnp.arange(TOKENS, dtype=jnp.int32) // TOK_DEV) % N_EXPERT).astype(jnp.int32)
    flat_index = (expert_ids * SLOTS + source[:, None] * MOST + slot_index).astype(jnp.int32)
    logits = jnp.dot(activations, router_weight.T, preferred_element_type=jnp.float32)
    onehot_f = onehot.astype(jnp.float32)
    chosen = jnp.sum(onehot_f * logits[:, None, :], axis=2)
    score = jax.nn.sigmoid(chosen)
    total = jnp.sum(score, axis=1, keepdims=True)
    group_index = flat_index.reshape(GROUPS, -1, TOPK)
    group_grad = out_grad.reshape(GROUPS, -1, D)

    def one_group(inputs):
        index_g, grad_g, saved_g = inputs
        picked = jnp.take(saved_g.reshape(EXPERTS * SLOTS, D), index_g, axis=0)
        return jnp.sum(grad_g.astype(jnp.float32)[:, None, :] * picked.astype(jnp.float32), axis=2)

    gate_dots = lax.map(one_group, (group_index, group_grad, saved_output)).reshape(TOKENS, TOPK)
    mean_term = jnp.sum(score * gate_dots, axis=1, keepdims=True) / total
    score_grad = route_scale / total * (gate_dots - mean_term) * score * (1.0 - score)
    grad_low = score_grad.astype(jnp.bfloat16)
    dense = jnp.sum(onehot_f * grad_low.astype(jnp.float32)[:, :, None], axis=1).astype(jnp.bfloat16)
    input_grad = jnp.dot(dense, router_weight, preferred_element_type=jnp.float32).astype(jnp.bfloat16)
    router_grad = jnp.dot(dense.T, activations, preferred_element_type=jnp.float32)
    return input_grad, score_grad, router_grad
```

```python
import jax
import jax.numpy as jnp
from jax import lax
from jax.experimental import pallas as pl
from jax.experimental.pallas import tpu as pltpu
from jax.sharding import Mesh, PartitionSpec as P

route_scale = 2.5
BF16, F32 = jnp.bfloat16, jnp.float32
NT = (((1,), (1,)), ((), ()))
TN = (((0,), (0,)), ((), ()))


def iota(shape, dim):
    return lax.broadcasted_iota(jnp.int32, shape, dim)


def pack_kernel(saved_steps, saved_ref, weight_ref, out_ref):
    rows, block = out_ref.shape
    experts, width = weight_ref.shape
    capacity = rows // (rows // (2 * experts)) // experts
    owners = rows // (experts * capacity)
    step = pl.program_id(0)
    row = iota((rows, rows), 0)
    col = iota((rows, rows), 1)

    @pl.when(step < saved_steps)
    def _():
        dest = row // (experts * capacity)
        local = row % (experts * capacity)
        source = (local // capacity) * (owners * capacity) + dest * capacity + local % capacity
        pick = (col == source).astype(F32).astype(BF16)
        out_ref[...] = jnp.dot(pick, saved_ref[...], preferred_element_type=F32).astype(BF16)

    for part in range(width // 2 // block):

        @pl.when(step == saved_steps + part)
        def _(part=part):
            r = iota((rows, experts), 0)
            e = iota((rows, experts), 1)
            total = jnp.zeros((rows, block), F32)
            for half in range(2):
                pick = (r % (2 * experts) == 2 * e + half).astype(F32).astype(BF16)
                piece = weight_ref[:, pl.ds(half * (width // 2) + part * block, block)]
                total += jnp.dot(pick, piece, preferred_element_type=F32)
            out_ref[...] = total.astype(BF16)


def pack(saved, weight):
    rows, width = saved.shape
    block = width // 4
    steps = 4 + 2
    return pl.pallas_call(
        lambda *refs: pack_kernel(4, *refs),
        grid=(steps,),
        in_specs=[
            pl.BlockSpec((rows, block), lambda j: (0, jnp.minimum(j, 3))),
            pl.BlockSpec(weight.shape, lambda j: (0, 0)),
        ],
        out_specs=pl.BlockSpec((rows, block), lambda j: (0, j)),
        out_shape=jax.ShapeDtypeStruct((rows, steps * block), BF16),
        name="pack_rows",
    )(saved, weight)


def score_kernel(ids_ref, got_ref, act_ref, grad_ref, score_grad_ref, spread_ref, part_ref):
    rows = got_ref.shape[0]
    tokens, width = act_ref.shape
    half = width // 2
    quarter = width // 4
    ids = ids_ref[...]
    col = iota((rows, tokens), 0)
    odd = (col % 2).astype(F32)
    named = [(col // 2 == ids[k : k + 1, :]) for k in range(2)]
    both = jnp.where(named[0] | named[1], 1.0, 0.0).astype(BF16)
    before = (iota((tokens, tokens), 0) < iota((tokens, tokens), 1)).astype(F32).astype(BF16)
    earlier = jnp.dot(both, before, preferred_element_type=F32)
    dots = lax.dot_general(got_ref[:, :width], grad_ref[...], NT, preferred_element_type=F32)
    dots = jnp.where(earlier == odd, dots, 0.0)
    low = lax.dot_general(
        got_ref[:, width:], act_ref[:, :half], NT, preferred_element_type=F32
    )
    high = lax.dot_general(
        got_ref[:, width:], act_ref[:, half:], NT, preferred_element_type=F32
    )
    logits = jnp.where(odd == 1.0, high, low)
    score, gate = [], []
    for k in range(2):
        chosen = jnp.sum(jnp.where(named[k], logits, 0.0), axis=0, keepdims=True)
        score.append(jax.nn.sigmoid(chosen))
        gate.append(jnp.sum(jnp.where(named[k], dots, 0.0), axis=0, keepdims=True))
    total = score[0] + score[1]
    mean_term = (score[0] * gate[0] + score[1] * gate[1]) / total
    dense = jnp.zeros((rows, tokens), F32)
    for k in range(2):
        grad = route_scale / total * (gate[k] - mean_term) * score[k] * (1.0 - score[k])
        score_grad_ref[k : k + 1, :] = grad
        dense = jnp.where(named[k], grad, dense)
    even_part = jnp.where(odd == 0.0, dense, 0.0).astype(BF16)
    odd_part = jnp.where(odd == 1.0, dense, 0.0).astype(BF16)
    spread_ref[:rows, :] = even_part
    spread_ref[rows:, :] = odd_part
    for side in range(2):
        out = jnp.dot(
            even_part,
            act_ref[:, side * half : side * half + quarter],
            preferred_element_type=F32,
        ) + jnp.dot(
            odd_part,
            act_ref[:, side * half + quarter : (side + 1) * half],
            preferred_element_type=F32,
        )
        part_ref[side * rows : (side + 1) * rows, :] = out.astype(BF16)


def scores(ids, got, act, grad):
    rows = got.shape[0]
    tokens, width = act.shape
    return pl.pallas_call(
        score_kernel,
        out_shape=(
            jax.ShapeDtypeStruct((2, tokens), F32),
            jax.ShapeDtypeStruct((2 * rows, tokens), BF16),
            jax.ShapeDtypeStruct((2 * rows, width // 4), BF16),
        ),
        compiler_params=pltpu.CompilerParams(vmem_limit_bytes=40 * 1024 * 1024),
        name="scores",
    )(ids, got, act, grad)


def input_kernel(spread_ref, weight_ref, out_ref):
    out_ref[...] = lax.dot_general(
        spread_ref[...], weight_ref[...], TN, preferred_element_type=F32
    ).astype(BF16)


def input_grads(spread, got, width):
    rows = got.shape[0]
    tokens = spread.shape[1]
    block = width // 4
    return pl.pallas_call(
        input_kernel,
        grid=(4,),
        in_specs=[
            pl.BlockSpec((rows, tokens), lambda j: (j // 2, 0)),
            pl.BlockSpec((rows, block), lambda j: (0, 4 + j % 2)),
        ],
        out_specs=pl.BlockSpec((tokens, block), lambda j: (0, j)),
        out_shape=jax.ShapeDtypeStruct((tokens, width), BF16),
        cost_estimate=pl.CostEstimate(
            flops=2 * tokens * rows * width, bytes_accessed=4 * tokens * width, transcendentals=0
        ),
        name="input_grads",
    )(spread, got)


def sum_kernel(got_ref, out_ref):
    rows, sources = out_ref.shape[0], got_ref.shape[0]
    pick = (iota((rows, sources), 0) % 8 == iota((rows, sources), 1) % 8).astype(F32).astype(BF16)
    out_ref[...] = jnp.dot(pick, got_ref[...], preferred_element_type=F32).astype(BF16)


def final_kernel(got_ref, out_ref):
    experts, width = out_ref.shape
    sources, block = got_ref.shape
    row = iota((experts, sources), 0)
    col = iota((experts, sources), 1) % (4 * experts)
    for piece in range(width // block):
        want = (piece // 2) * 2 * experts + row * 2 + piece % 2
        pick = (col == want).astype(F32).astype(BF16)
        out_ref[:, piece * block : (piece + 1) * block] = jnp.dot(
            pick, got_ref[...], preferred_element_type=F32
        )


def body(activations, out_grad, router_weight, expert_ids, saved_output):
    experts, width = router_weight.shape
    planes = lax.axis_size("pairs") * lax.axis_size("side")
    saved = saved_output.reshape(experts * saved_output.shape[2], width)
    packed = pack(saved, router_weight)
    got = lax.all_to_all(packed, "expert", split_axis=0, concat_axis=0, tiled=True)
    score_grad, spread, part = scores(expert_ids.T, got, activations, out_grad)
    part = lax.all_to_all(part, ("side", "expert"), split_axis=0, concat_axis=0, tiled=True)
    input_grad = input_grads(spread, got, width)
    rows = 2 * experts
    summed = pl.pallas_call(
        sum_kernel,
        out_shape=jax.ShapeDtypeStruct((planes * rows, width // 4), BF16),
        name="sum_planes",
    )(part)
    summed = lax.all_to_all(summed, ("pairs", "side"), split_axis=0, concat_axis=0, tiled=True)
    router_grad = pl.pallas_call(
        final_kernel,
        out_shape=jax.ShapeDtypeStruct((experts, width), F32),
        name="sum_batches",
    )(summed)
    return input_grad, score_grad.T, router_grad


def solution(mesh):
    dp, owners = mesh.shape["dp"], mesh.shape["expert"]
    mesh = Mesh(mesh.devices.reshape(dp // 2, 2, owners), ("pairs", "side", "expert"))
    tokens = P(("pairs", "side", "expert"), None)
    in_specs = (
        tokens,
        tokens,
        P("expert", None),
        tokens,
        P(("pairs", "side"), "expert", None, None),
    )
    out_specs = (tokens, tokens, P("expert", None))
    return jax.shard_map(body, mesh=mesh, in_specs=in_specs, out_specs=out_specs, check_vma=False)
```

```python
import jax
import jax.numpy as jnp
from jax import lax
from jax.experimental import pallas as pl
from jax.experimental.pallas import tpu as pltpu
from jax.sharding import Mesh, PartitionSpec as P

route_scale = 2.5
BF16, F32 = jnp.bfloat16, jnp.float32
NT = (((1,), (1,)), ((), ()))
TN = (((0,), (0,)), ((), ()))
BIG = pltpu.CompilerParams(vmem_limit_bytes=40 * 1024 * 1024)


def iota(shape, dim):
    return lax.broadcasted_iota(jnp.int32, shape, dim)


def ones_where(mask):
    return jnp.where(mask, 1.0, 0.0).astype(BF16)


def pack_kernel(saved_hbm, weight_hbm, out_ref, saved_ref, weight_ref, saved_sem, weight_sem):
    rows, width = saved_ref.shape
    half = width // 2
    blocks = [slice(h * half, (h + 1) * half) for h in range(2)]
    copies = [
        pltpu.make_async_copy(saved_hbm.at[:, block], saved_ref.at[:, block], saved_sem.at[h])
        for h, block in enumerate(blocks)
    ]
    copies.append(pltpu.make_async_copy(weight_hbm, weight_ref, weight_sem))
    for copy in copies:
        copy.start()
    row, col = iota((rows, rows), 0), iota((rows, rows), 1)
    pick = ones_where(col == ((row >> 1) & 3) * (rows // 4) + (row >> 3) * 2 + (row & 1))
    row, col = iota((rows, 8), 0), iota((rows, 8), 1)
    pick_weight = ones_where(col == ((row >> 1) & 3) + (row & 1) * 4)
    copies[2].wait()
    halves = jnp.concatenate([weight_ref[:, block] for block in blocks], axis=0)
    out_ref[:, width:] = jnp.dot(pick_weight, halves, preferred_element_type=F32).astype(BF16)
    for h, block in enumerate(blocks):
        copies[h].wait()
        out_ref[:, block] = jnp.dot(
            pick, saved_ref[:, block], preferred_element_type=F32
        ).astype(BF16)


def pack(saved, weight):
    rows, width = saved.shape
    return pl.pallas_call(
        pack_kernel,
        in_specs=[pl.BlockSpec(memory_space=pltpu.HBM)] * 2,
        out_shape=jax.ShapeDtypeStruct((rows, width + width // 2), BF16),
        scratch_shapes=[
            pltpu.VMEM((rows, width), BF16),
            pltpu.VMEM(weight.shape, BF16),
            pltpu.SemaphoreType.DMA((2,)),
            pltpu.SemaphoreType.DMA,
        ],
        compiler_params=BIG,
        name="pack_rows",
    )(*[pltpu.with_memory_space_constraint(a, pltpu.HBM) for a in (saved, weight)])


def named_rows(ids, rows):
    row = iota((rows, ids.shape[1]), 0)
    return [(row >> 1) == ids[k : k + 1, :] for k in range(2)]


def score_kernel(ids_ref, got_ref, act_ref, grad_ref, score_grad_ref, part_ref):
    rows = got_ref.shape[0]
    tokens, width = act_ref.shape
    half, quarter = width // 2, width // 4
    ids = ids_ref[...]
    named = named_rows(ids, rows)
    odd = (iota((rows, tokens), 0) & 1) == 1
    before = ones_where(iota((tokens, tokens), 0) < iota((tokens, tokens), 1))
    earlier = jnp.dot(ones_where(named[0] | named[1]), before, preferred_element_type=F32)
    dots = lax.dot_general(got_ref[:, :width], grad_ref[...], NT, preferred_element_type=F32)
    dots = jnp.where(earlier == jnp.where(odd, 1.0, 0.0), dots, 0.0)
    halves = jnp.concatenate([act_ref[:, :half], act_ref[:, half:]], axis=0)
    logits = lax.dot_general(got_ref[:, width:], halves, NT, preferred_element_type=F32)
    logits = jnp.where(odd, logits[:, tokens:], logits[:, :tokens])
    score, gate = [], []
    for k in range(2):
        chosen = jnp.sum(jnp.where(named[k], logits, 0.0), axis=0, keepdims=True)
        score.append(jax.nn.sigmoid(chosen))
        gate.append(jnp.sum(jnp.where(named[k], dots, 0.0), axis=0, keepdims=True))
    total = score[0] + score[1]
    mean_term = (score[0] * gate[0] + score[1] * gate[1]) / total
    dense = jnp.zeros((rows, tokens), F32)
    for k in range(2):
        grad = route_scale / total * (gate[k] - mean_term) * score[k] * (1.0 - score[k])
        score_grad_ref[k : k + 1, :] = grad
        dense = jnp.where(named[k], grad, dense)
    sides = [jnp.where(odd, 0.0, dense).astype(BF16), jnp.where(odd, dense, 0.0).astype(BF16)]
    sides = jnp.concatenate(sides, axis=1)
    for side in range(2):
        columns = act_ref[:, side * half : (side + 1) * half]
        pair = jnp.concatenate([columns[:, :quarter], columns[:, quarter:]], axis=0)
        part_ref[side * rows : (side + 1) * rows, :] = jnp.dot(
            sides, pair, preferred_element_type=F32
        ).astype(BF16)


def input_kernel(ids_ref, score_grad_ref, got_ref, out_ref):
    rows = got_ref.shape[0]
    tokens, width = out_ref.shape
    half = width // 2
    named = named_rows(ids_ref[...], rows)
    odd = (iota((rows, tokens), 0) & 1) == 1
    dense = jnp.zeros((rows, tokens), F32)
    for k in range(2):
        dense = jnp.where(named[k], score_grad_ref[k : k + 1, :], dense)
    for h in range(2):
        picked = jnp.where(odd == (h == 1), dense, 0.0).astype(BF16)
        out_ref[:, h * half : (h + 1) * half] = lax.dot_general(
            picked, got_ref[:, width:], TN, preferred_element_type=F32
        ).astype(BF16)


def sum_kernel(got_ref, out_ref):
    rows, sources = out_ref.shape[0], got_ref.shape[0]
    pick = ones_where((iota((rows, sources), 0) & 7) == (iota((rows, sources), 1) & 7))
    out_ref[...] = jnp.dot(pick, got_ref[...], preferred_element_type=F32).astype(BF16)


def final_kernel(got_ref, out_ref):
    experts = out_ref.shape[0]
    sources, block = got_ref.shape
    row, col = iota((experts, sources), 0), iota((experts, sources), 1)
    for piece in range(4):
        pick = ones_where((col & 15) == ((piece >> 1) * 8 + row * 2 + (piece & 1)))
        out_ref[:, piece * block : (piece + 1) * block] = jnp.dot(
            pick, got_ref[...], preferred_element_type=F32
        )


def call(kernel, name, out_shape, *args, cost=None):
    return pl.pallas_call(
        kernel, out_shape=out_shape, compiler_params=BIG, cost_estimate=cost, name=name
    )(*args)


def body(activations, out_grad, router_weight, expert_ids, saved_output):
    experts, width = router_weight.shape
    tokens = activations.shape[0]
    planes = lax.axis_size("pairs") * lax.axis_size("side")
    rows = experts * saved_output.shape[2]
    ids = expert_ids.T
    packed = pack(saved_output.reshape(rows, width), router_weight)
    got = lax.all_to_all(packed, "expert", split_axis=0, concat_axis=0, tiled=True)
    score_grad, part = call(
        score_kernel,
        "scores",
        (
            jax.ShapeDtypeStruct((2, tokens), F32),
            jax.ShapeDtypeStruct((2 * rows, width // 4), BF16),
        ),
        ids,
        got,
        activations,
        out_grad,
    )
    part = lax.all_to_all(part, ("side", "expert"), split_axis=0, concat_axis=0, tiled=True)
    input_grad = call(
        input_kernel,
        "input_grads",
        jax.ShapeDtypeStruct((tokens, width), BF16),
        ids,
        score_grad,
        got,
        cost=pl.CostEstimate(
            flops=2 * tokens * rows * width, bytes_accessed=4 * tokens * width, transcendentals=0
        ),
    )
    summed = call(
        sum_kernel,
        "sum_planes",
        jax.ShapeDtypeStruct((planes * 2 * experts, width // 4), BF16),
        part,
    )
    summed = lax.all_to_all(summed, ("pairs", "side"), split_axis=0, concat_axis=0, tiled=True)
    router_grad = call(
        final_kernel, "sum_batches", jax.ShapeDtypeStruct((experts, width), F32), summed
    )
    return input_grad, score_grad.T, router_grad


def solution(mesh):
    dp, owners = mesh.shape["dp"], mesh.shape["expert"]
    mesh = Mesh(mesh.devices.reshape(dp // 2, 2, owners), ("pairs", "side", "expert"))
    tokens = P(("pairs", "side", "expert"), None)
    in_specs = (
        tokens,
        tokens,
        P("expert", None),
        tokens,
        P(("pairs", "side"), "expert", None, None),
    )
    out_specs = (tokens, tokens, P("expert", None))
    return jax.shard_map(body, mesh=mesh, in_specs=in_specs, out_specs=out_specs, check_vma=False)
```

```python
import jax
import jax.numpy as jnp
from jax import lax
from jax.experimental import pallas as pl
from jax.experimental.pallas import tpu as pltpu
from jax.sharding import Mesh, PartitionSpec as P

route_scale = 2.5
BF16, F32 = jnp.bfloat16, jnp.float32
NT = (((1,), (1,)), ((), ()))
TN = (((0,), (0,)), ((), ()))
WIDE = 512
BIG = pltpu.CompilerParams(vmem_limit_bytes=40 * 1024 * 1024)


def iota(shape, dim):
    return lax.broadcasted_iota(jnp.int32, shape, dim)


def ones_where(mask):
    return jnp.where(mask, 1.0, 0.0).astype(BF16)


def pack_kernel(saved_hbm, weight_hbm, out_hbm, saved_ref, weight_ref, out_ref, in_sem, out_sem):
    rows, width = saved_ref.shape
    half, quarter, per_core = width // 2, width // 4, rows // 2
    halves = [slice(k * half, (k + 1) * half) for k in range(2)]
    copies = [
        pltpu.make_async_copy(saved_hbm.at[:, block], saved_ref.at[:, block], in_sem.at[k])
        for k, block in enumerate(halves)
    ]
    copies.append(pltpu.make_async_copy(weight_hbm, weight_ref, in_sem.at[2]))
    for copy in copies:
        copy.start()
    row, col = iota((rows, rows), 0), iota((rows, rows), 1)
    local = row & (per_core - 1)
    source = ((local >> 1) & 3) * (rows // 4) + (local >> 3) * 4 + (local & 1)
    pick = ones_where(col == source + jnp.where(row < per_core, 0, 2))
    row, col = iota((per_core, 8), 0), iota((per_core, 8), 1)
    pick_weight = ones_where(col == ((row >> 1) & 3) + (row & 1) * 4)
    copies[2].wait()
    sent = []
    for k, block in enumerate(halves):
        mine = slice(k * per_core, (k + 1) * per_core)
        parts = [
            weight_ref[:, k * half + m * quarter : k * half + (m + 1) * quarter] for m in range(2)
        ]
        out_ref[mine, width:] = jnp.dot(
            pick_weight, jnp.concatenate(parts, axis=0), preferred_element_type=F32
        ).astype(BF16)
        copies[k].wait()
        out = jnp.dot(pick, saved_ref[:, block], preferred_element_type=F32).astype(BF16)
        for core in range(2):
            out_ref[mine, halves[core]] = out[core * per_core : (core + 1) * per_core]
        sent.append(pltpu.make_async_copy(out_ref.at[mine], out_hbm.at[mine], out_sem.at[k]))
        sent[k].start()
    for copy in sent:
        copy.wait()


def pack(saved, weight):
    rows, width = saved.shape
    packed = (rows, width + width // 4)
    return pl.pallas_call(
        pack_kernel,
        in_specs=[pl.BlockSpec(memory_space=pltpu.HBM)] * 2,
        out_specs=pl.BlockSpec(memory_space=pltpu.HBM),
        out_shape=pltpu.HBM(packed, BF16),
        scratch_shapes=[
            pltpu.VMEM((rows, width), BF16),
            pltpu.VMEM(weight.shape, BF16),
            pltpu.VMEM(packed, BF16),
            pltpu.SemaphoreType.DMA((3,)),
            pltpu.SemaphoreType.DMA((2,)),
        ],
        compiler_params=BIG,
        name="pack_rows",
    )(in_hbm(saved), in_hbm(weight))


def in_hbm(array):
    return pltpu.with_memory_space_constraint(array, pltpu.HBM)


def half_copies(core, act_hbm, grad_hbm, out_ref, sem):
    tokens, half = act_hbm.shape[0], act_hbm.shape[1] // 2
    block = pl.ds(pl.multiple_of(core * half, 128), half)
    return [
        pltpu.make_async_copy(
            array.at[:, block], out_ref.at[pl.ds(i * tokens, tokens)], sem.at[i]
        )
        for i, array in enumerate((act_hbm, grad_hbm))
    ]


def halves_kernel(core_ref, act_hbm, grad_hbm, out_ref, sem):
    copies = half_copies(1 - core_ref[0], act_hbm, grad_hbm, out_ref, sem)
    for copy in copies:
        copy.start()
    for copy in copies:
        copy.wait()


def halves_for_other(core, act, grad):
    tokens, width = act.shape
    return pl.pallas_call(
        halves_kernel,
        in_specs=[pl.BlockSpec(memory_space=pltpu.SMEM)]
        + [pl.BlockSpec(memory_space=pltpu.HBM)] * 2,
        out_shape=jax.ShapeDtypeStruct((2 * tokens, width // 2), BF16),
        scratch_shapes=[pltpu.SemaphoreType.DMA((2,))],
        compiler_params=BIG,
        name="halves_for_other",
    )(core, in_hbm(act), in_hbm(grad))


def named_rows(ids, rows):
    row = iota((rows, ids.shape[1]), 0)
    chips = rows // 16
    expert = ((row >> 3) & (chips - 1)) * 8 + (row >= rows // 2) * 4 + ((row >> 1) & 3)
    return [expert == ids[k : k + 1, :] for k in range(2)]


def odd_rows(rows, tokens):
    return (iota((rows, tokens), 0) & 1) == 1


def dots_kernel(
    core_ref, ids_ref, other_ids_ref, other_ref, got_ref, act_hbm, grad_hbm, out_ref, own_ref, sem
):
    rows = got_ref.shape[0]
    tokens, half = own_ref.shape[0] // 2, own_ref.shape[1]
    quarter = half // 2
    core = core_ref[0]
    copies = half_copies(core, act_hbm, grad_hbm, own_ref, sem)
    for copy in copies:
        copy.start()
    odd = odd_rows(rows, tokens)
    before = ones_where(iota((tokens, tokens), 0) < iota((tokens, tokens), 1))
    for owner, ids, halves_ref in (
        (1 - core, other_ids_ref[...], other_ref),
        (core, ids_ref[...], own_ref),
    ):
        if halves_ref is own_ref:
            for copy in copies:
                copy.wait()
        saved = got_ref[:, pl.ds(pl.multiple_of(owner * half, 128), half)]
        dots = lax.dot_general(
            saved, halves_ref[tokens:, :], NT, preferred_element_type=F32
        )
        named = named_rows(ids, rows)
        earlier = jnp.dot(ones_where(named[0] | named[1]), before, preferred_element_type=F32)
        dots = jnp.where(earlier == jnp.where(odd, 1.0, 0.0), dots, 0.0)
        parts = [halves_ref[:tokens, :quarter], halves_ref[:tokens, quarter:]]
        logits = lax.dot_general(
            got_ref[:, 2 * half :],
            jnp.concatenate(parts, axis=0),
            NT,
            preferred_element_type=F32,
        )
        logits = jnp.where(odd, logits[:, tokens:], logits[:, :tokens])
        sums = [
            jnp.sum(jnp.where(named[k], values, 0.0), axis=0, keepdims=True)
            for values in (dots, logits)
            for k in range(2)
        ]
        sums.append(jnp.zeros((4, tokens), F32))
        out_ref[pl.ds(pl.multiple_of(owner * 8, 8), 8), :] = jnp.concatenate(sums, axis=0)


def gate_dots(core, ids, other_ids, other, got, act, grad):
    tokens = act.shape[0]
    vmem, hbm = pl.BlockSpec(memory_space=pltpu.VMEM), pl.BlockSpec(memory_space=pltpu.HBM)
    return pl.pallas_call(
        dots_kernel,
        in_specs=[pl.BlockSpec(memory_space=pltpu.SMEM)] + [vmem] * 4 + [hbm] * 2,
        out_shape=(
            jax.ShapeDtypeStruct((16, tokens), F32),
            jax.ShapeDtypeStruct(other.shape, BF16),
        ),
        scratch_shapes=[pltpu.SemaphoreType.DMA((2,))],
        compiler_params=BIG,
        name="gate_dots",
    )(core, ids, other_ids, other, got, in_hbm(act), in_hbm(grad))


def score_kernel(
    core_ref, mine_ref, theirs_ref, ids_ref, other_ids_ref, own_ref, other_ref, *outs
):
    score_grad_ref, part_ref = outs
    rows, wide = part_ref.shape[0] // 2, part_ref.shape[1]
    tokens, quarter = own_ref.shape[0] // 2, own_ref.shape[1] // 2
    core = core_ref[0]
    odd = odd_rows(rows, tokens)
    left = []
    for owner, ids in ((core, ids_ref[...]), (1 - core, other_ids_ref[...])):
        block = pl.ds(pl.multiple_of(owner * 8, 8), 8)
        sums = mine_ref[block, :] + theirs_ref[block, :]
        gate = [sums[k : k + 1, :] for k in range(2)]
        score = [jax.nn.sigmoid(sums[2 + k : 3 + k, :]) for k in range(2)]
        total = score[0] + score[1]
        mean_term = (score[0] * gate[0] + score[1] * gate[1]) / total
        named = named_rows(ids, rows)
        dense = jnp.zeros((rows, tokens), F32)
        for k in range(2):
            grad = route_scale / total * (gate[k] - mean_term) * score[k] * (1.0 - score[k])
            if not left:
                score_grad_ref[k : k + 1, :] = grad
            dense = jnp.where(named[k], grad, dense)
        left += [jnp.where(odd, 0.0, dense).astype(BF16), jnp.where(odd, dense, 0.0).astype(BF16)]
    left = jnp.concatenate(left, axis=1)
    rest = jnp.zeros((tokens, 2 * wide - quarter), BF16)
    for side in range(2):
        right = []
        for halves_ref in (own_ref, other_ref):
            act = halves_ref[:tokens, side * quarter : (side + 1) * quarter]
            right += [act[:, :wide], jnp.concatenate([act[:, wide:], rest], axis=1)]
        part_ref[side * rows : (side + 1) * rows, :] = jnp.dot(
            left, jnp.concatenate(right, axis=0), preferred_element_type=F32
        ).astype(BF16)


def input_kernel(core_ref, ids_ref, score_grad_ref, own_ref, other_ref, out_ref):
    rows, quarter = own_ref.shape
    tokens = out_ref.shape[0]
    odd = odd_rows(rows, tokens)
    named = named_rows(ids_ref[...], rows)
    dense = jnp.zeros((rows, tokens), F32)
    for k in range(2):
        dense = jnp.where(named[k], score_grad_ref[k : k + 1, :], dense)
    for m in range(2):
        picked = jnp.where(odd == (m == 1), dense, 0.0).astype(BF16)
        for core, weight_ref in ((core_ref[0], own_ref), (1 - core_ref[0], other_ref)):
            block = pl.ds(pl.multiple_of((core * 2 + m) * quarter, 128), quarter)
            out_ref[:, block] = lax.dot_general(
                picked, weight_ref[...], TN, preferred_element_type=F32
            ).astype(BF16)


def sum_kernel(got_ref, out_ref):
    rows, sources = out_ref.shape[0], got_ref.shape[0]
    wide, columns = got_ref.shape[1], out_ref.shape[1]
    row, col = iota((rows, sources), 0), iota((rows, sources), 1)
    sent_by = (col & (sources // 2 - 1)) >= sources // 4
    same = (row & 7) == jnp.where(sent_by, 4, 0) + ((col >> 1) & 3)
    for h in range(2):
        pick = ones_where(same & ((col & 1) == h))
        start = h * wide
        count = wide if h == 0 else columns - wide
        out_ref[:, start : start + count] = jnp.dot(
            pick, got_ref[:, :count], preferred_element_type=F32
        ).astype(BF16)


def final_kernel(got_ref, out_ref):
    experts = out_ref.shape[0]
    sources, quarter = got_ref.shape
    row, col = iota((experts, sources), 0), iota((experts, sources), 1)
    for half in range(2):
        for side in range(2):
            pick = ones_where((col & 15) == side * 8 + half * 4 + row)
            start = (half * 2 + side) * quarter
            out_ref[:, start : start + quarter] = jnp.dot(
                pick, got_ref[...], preferred_element_type=F32
            )


def call(kernel, name, out_shape, *args, cost=None):
    return pl.pallas_call(
        kernel,
        in_specs=[
            pl.BlockSpec(memory_space=pltpu.SMEM if a.shape == (1,) else pltpu.VMEM) for a in args
        ],
        out_shape=out_shape,
        compiler_params=BIG,
        cost_estimate=cost,
        name=name,
    )(*args)


def body(activations, out_grad, router_weight, expert_ids, saved_output):
    experts, width = router_weight.shape
    tokens = activations.shape[0]
    planes = lax.axis_size("pairs") * lax.axis_size("side")
    rows = experts * saved_output.shape[2]
    core = lax.axis_index("core").astype(jnp.int32).reshape(1)
    ids = expert_ids.T

    def swap(x):
        return lax.ppermute(x, "core", [(0, 1), (1, 0)])

    packed = pack(saved_output.reshape(rows, width), router_weight)
    got = lax.all_to_all(packed, ("core", "chip"), split_axis=0, concat_axis=0, tiled=True)
    other = swap(halves_for_other(core, activations, out_grad))
    other_ids = swap(ids)
    mine, own = gate_dots(core, ids, other_ids, other, got, activations, out_grad)
    score_grad, part = call(
        score_kernel,
        "scores",
        (
            jax.ShapeDtypeStruct((2, tokens), F32),
            jax.ShapeDtypeStruct((2 * rows, WIDE), BF16),
        ),
        core,
        mine,
        swap(mine),
        ids,
        other_ids,
        own,
        other,
    )
    part = lax.all_to_all(
        part, ("side", "core", "chip"), split_axis=0, concat_axis=0, tiled=True
    )
    summed = call(
        sum_kernel,
        "sum_owners",
        jax.ShapeDtypeStruct((planes * 2 * experts, width // 4), BF16),
        part,
    )
    got, summed = lax.optimization_barrier((got, summed))
    weight = got[:, width:]
    input_grad = call(
        input_kernel,
        "input_grads",
        jax.ShapeDtypeStruct((tokens, width), BF16),
        core,
        ids,
        score_grad,
        weight,
        swap(weight),
        cost=pl.CostEstimate(
            flops=2 * tokens * rows * width, bytes_accessed=4 * tokens * width, transcendentals=0
        ),
    )
    summed = lax.all_to_all(summed, ("pairs", "side"), split_axis=0, concat_axis=0, tiled=True)
    router_grad = call(
        final_kernel, "sum_batches", jax.ShapeDtypeStruct((experts, width), F32), summed
    )
    return input_grad, score_grad.T, router_grad


def solution(mesh):
    dp, owners = mesh.shape["dp"], mesh.shape["expert"]
    devices = mesh.devices.reshape(dp // 2, 2, owners // 2, 2)
    mesh = Mesh(devices, ("pairs", "side", "chip", "core"))
    tokens = P(("pairs", "side", "chip", "core"), None)
    in_specs = (
        tokens,
        tokens,
        P(("chip", "core"), None),
        tokens,
        P(("pairs", "side"), ("chip", "core"), None, None),
    )
    out_specs = (tokens, tokens, P(("chip", "core"), None))
    return jax.shard_map(body, mesh=mesh, in_specs=in_specs, out_specs=out_specs, check_vma=False)
```

```python
import jax
import jax.numpy as jnp
from jax import lax
from jax.experimental import pallas as pl
from jax.experimental.pallas import tpu as pltpu
from jax.sharding import Mesh, PartitionSpec as P

route_scale = 2.5
BF16, F32 = jnp.bfloat16, jnp.float32
NT = (((1,), (1,)), ((), ()))
TN = (((0,), (0,)), ((), ()))
BIG = pltpu.CompilerParams(vmem_limit_bytes=40 * 1024 * 1024)


def iota(shape, dim):
    return lax.broadcasted_iota(jnp.int32, shape, dim)


def ones_where(mask):
    return jnp.where(mask, 1.0, 0.0).astype(BF16)


def pack_kernel(saved_hbm, weight_hbm, out_hbm, saved_ref, weight_ref, out_ref, in_sem, out_sem):
    rows, width = saved_ref.shape
    half, quarter, per_core = width // 2, width // 4, rows // 2
    halves = [slice(k * half, (k + 1) * half) for k in range(2)]
    copies = [
        pltpu.make_async_copy(saved_hbm.at[:, block], saved_ref.at[:, block], in_sem.at[k])
        for k, block in enumerate(halves)
    ]
    copies.append(pltpu.make_async_copy(weight_hbm, weight_ref, in_sem.at[2]))
    for i in (0, 2, 1):
        copies[i].start()
    row, col = iota((rows, rows), 0), iota((rows, rows), 1)
    local = row & (per_core - 1)
    source = ((local >> 1) & 3) * (rows // 4) + (local >> 3) * 4 + (local & 1)
    pick = ones_where(col == source + jnp.where(row < per_core, 0, 2))
    row, col = iota((per_core, 8), 0), iota((per_core, 8), 1)
    pick_weight = ones_where(col == ((row >> 1) & 3) + (row & 1) * 4)
    copies[2].wait()
    sent = []
    for k, block in enumerate(halves):
        mine = slice(k * per_core, (k + 1) * per_core)
        parts = [
            weight_ref[:, k * half + m * quarter : k * half + (m + 1) * quarter] for m in range(2)
        ]
        out_ref[mine, width:] = jnp.dot(
            pick_weight, jnp.concatenate(parts, axis=0), preferred_element_type=F32
        ).astype(BF16)
        copies[k].wait()
        out = jnp.dot(pick, saved_ref[:, block], preferred_element_type=F32).astype(BF16)
        for core in range(2):
            out_ref[mine, halves[core]] = out[core * per_core : (core + 1) * per_core]
        sent.append(pltpu.make_async_copy(out_ref.at[mine], out_hbm.at[mine], out_sem.at[k]))
        sent[k].start()
    for copy in sent:
        copy.wait()


def pack(saved, weight):
    rows, width = saved.shape
    packed = (rows, width + width // 4)
    return pl.pallas_call(
        pack_kernel,
        in_specs=[pl.BlockSpec(memory_space=pltpu.HBM)] * 2,
        out_specs=pl.BlockSpec(memory_space=pltpu.HBM),
        out_shape=pltpu.HBM(packed, BF16),
        scratch_shapes=[
            pltpu.VMEM((rows, width), BF16),
            pltpu.VMEM(weight.shape, BF16),
            pltpu.VMEM(packed, BF16),
            pltpu.SemaphoreType.DMA((3,)),
            pltpu.SemaphoreType.DMA((2,)),
        ],
        compiler_params=BIG,
        name="pack_rows",
    )(in_hbm(saved), in_hbm(weight))


def in_hbm(array):
    return pltpu.with_memory_space_constraint(array, pltpu.HBM)


def half_copies(pieces, sems):
    copies = []
    for i, (array, half, out_ref) in enumerate(pieces):
        width = out_ref.shape[1]
        block = pl.ds(pl.multiple_of(half * width, 128), width)
        copies.append(pltpu.make_async_copy(array.at[:, block], out_ref, sems.at[i]))
    return copies


def halves_kernel(core_ref, act_hbm, grad_hbm, out_ref, rest_ref, sem):
    tokens = act_hbm.shape[0]
    mine, theirs = core_ref[0], 1 - core_ref[0]
    copies = half_copies(
        [
            (act_hbm, theirs, out_ref.at[pl.ds(0, tokens)]),
            (grad_hbm, theirs, out_ref.at[pl.ds(tokens, tokens)]),
            (act_hbm, mine, rest_ref),
        ],
        sem,
    )
    for copy in copies:
        copy.start()
    for copy in copies:
        copy.wait()


def halves_for_other(core, act, grad):
    tokens, width = act.shape
    return pl.pallas_call(
        halves_kernel,
        in_specs=[pl.BlockSpec(memory_space=pltpu.SMEM)]
        + [pl.BlockSpec(memory_space=pltpu.HBM)] * 2,
        out_shape=(
            jax.ShapeDtypeStruct((2 * tokens, width // 2), BF16),
            jax.ShapeDtypeStruct((tokens, width // 2), BF16),
        ),
        scratch_shapes=[pltpu.SemaphoreType.DMA((3,))],
        compiler_params=BIG,
        name="halves_for_other",
    )(core, in_hbm(act), in_hbm(grad))


def named_rows(ids, rows):
    row = iota((rows, ids.shape[1]), 0)
    chips = rows // 16
    expert = ((row >> 3) & (chips - 1)) * 8 + (row >= rows // 2) * 4 + ((row >> 1) & 3)
    return [expert == ids[k : k + 1, :] for k in range(2)]


def odd_rows(rows, tokens):
    return (iota((rows, tokens), 0) & 1) == 1


def dots_kernel(
    core_ref,
    ids_ref,
    other_ids_ref,
    other_ref,
    got_ref,
    other_rest_hbm,
    act_hbm,
    grad_hbm,
    out_ref,
    own_ref,
    rest_ref,
    sem,
):
    rows = got_ref.shape[0]
    tokens, half = own_ref.shape[0] // 2, own_ref.shape[1]
    quarter = half // 2
    core = core_ref[0]
    low, high = pl.ds(0, tokens), pl.ds(tokens, tokens)
    copies = half_copies(
        [
            (act_hbm, core, own_ref.at[low]),
            (grad_hbm, core, own_ref.at[high]),
            (act_hbm, 1 - core, rest_ref.at[low]),
            (other_rest_hbm, 0, rest_ref.at[high]),
        ],
        sem,
    )
    for copy in copies:
        copy.start()
    odd = odd_rows(rows, tokens)
    before = ones_where(iota((tokens, tokens), 0) < iota((tokens, tokens), 1))
    for owner, ids, halves_ref in (
        (1 - core, other_ids_ref[...], other_ref),
        (core, ids_ref[...], own_ref),
    ):
        if halves_ref is own_ref:
            for copy in copies[:2]:
                copy.wait()
        saved = got_ref[:, pl.ds(pl.multiple_of(owner * half, 128), half)]
        dots = lax.dot_general(
            saved, halves_ref[tokens:, :], NT, preferred_element_type=F32
        )
        named = named_rows(ids, rows)
        earlier = jnp.dot(ones_where(named[0] | named[1]), before, preferred_element_type=F32)
        dots = jnp.where(earlier == jnp.where(odd, 1.0, 0.0), dots, 0.0)
        parts = [halves_ref[:tokens, :quarter], halves_ref[:tokens, quarter:]]
        logits = lax.dot_general(
            got_ref[:, 2 * half :],
            jnp.concatenate(parts, axis=0),
            NT,
            preferred_element_type=F32,
        )
        logits = jnp.where(odd, logits[:, tokens:], logits[:, :tokens])
        sums = [
            jnp.sum(jnp.where(named[k], values, 0.0), axis=0, keepdims=True)
            for values in (dots, logits)
            for k in range(2)
        ]
        sums.append(jnp.zeros((4, tokens), F32))
        out_ref[pl.ds(pl.multiple_of(owner * 8, 8), 8), :] = jnp.concatenate(sums, axis=0)
    for copy in copies[2:]:
        copy.wait()


def gate_dots(core, ids, other_ids, other, got, other_rest, act, grad):
    tokens = act.shape[0]
    vmem, hbm = pl.BlockSpec(memory_space=pltpu.VMEM), pl.BlockSpec(memory_space=pltpu.HBM)
    return pl.pallas_call(
        dots_kernel,
        in_specs=[pl.BlockSpec(memory_space=pltpu.SMEM)] + [vmem] * 4 + [hbm] * 3,
        out_shape=(
            jax.ShapeDtypeStruct((16, tokens), F32),
            jax.ShapeDtypeStruct(other.shape, BF16),
            jax.ShapeDtypeStruct(other.shape, BF16),
        ),
        scratch_shapes=[pltpu.SemaphoreType.DMA((4,))],
        compiler_params=BIG,
        name="gate_dots",
    )(core, ids, other_ids, other, got, in_hbm(other_rest), in_hbm(act), in_hbm(grad))


def score_kernel(
    core_ref, mine_ref, theirs_ref, ids_ref, other_ids_ref, own_ref, other_ref, rest_ref, *outs
):
    score_grad_ref, part_ref = outs
    rows, quarter = part_ref.shape[0] // 2, part_ref.shape[1]
    tokens = ids_ref.shape[1]
    core = core_ref[0]
    odd = odd_rows(rows, tokens)
    row = iota((rows, tokens), 0)
    expert = (row >> 3) * 8 + core * 4 + ((row >> 1) & 3)
    left = []
    for owner, ids in ((core, ids_ref[...]), (1 - core, other_ids_ref[...])):
        block = pl.ds(pl.multiple_of(owner * 8, 8), 8)
        sums = mine_ref[block, :] + theirs_ref[block, :]
        gate = [sums[k : k + 1, :] for k in range(2)]
        score = [jax.nn.sigmoid(sums[2 + k : 3 + k, :]) for k in range(2)]
        total = score[0] + score[1]
        mean_term = (score[0] * gate[0] + score[1] * gate[1]) / total
        dense = jnp.zeros((rows, tokens), F32)
        for k in range(2):
            grad = route_scale / total * (gate[k] - mean_term) * score[k] * (1.0 - score[k])
            if not left:
                score_grad_ref[k : k + 1, :] = grad
            dense = jnp.where(expert == ids[k : k + 1, :], grad, dense)
        left += [jnp.where(odd, 0.0, dense).astype(BF16), jnp.where(odd, dense, 0.0).astype(BF16)]
    left = jnp.concatenate(left, axis=1)
    for side, acts in (
        (core, (own_ref[:tokens, :], other_ref[:tokens, :])),
        (1 - core, (rest_ref[:tokens, :], rest_ref[tokens:, :])),
    ):
        right = [act[:, h * quarter : (h + 1) * quarter] for act in acts for h in range(2)]
        part_ref[pl.ds(pl.multiple_of(side * rows, 16), rows), :] = jnp.dot(
            left, jnp.concatenate(right, axis=0), preferred_element_type=F32
        ).astype(BF16)


def input_kernel(core_ref, ids_ref, score_grad_ref, own_ref, other_ref, out_ref):
    rows, quarter = own_ref.shape
    tokens = out_ref.shape[0]
    odd = odd_rows(rows, tokens)
    named = named_rows(ids_ref[...], rows)
    dense = jnp.zeros((rows, tokens), F32)
    for k in range(2):
        dense = jnp.where(named[k], score_grad_ref[k : k + 1, :], dense)
    for m in range(2):
        picked = jnp.where(odd == (m == 1), dense, 0.0).astype(BF16)
        for core, weight_ref in ((core_ref[0], own_ref), (1 - core_ref[0], other_ref)):
            block = pl.ds(pl.multiple_of((core * 2 + m) * quarter, 128), quarter)
            out_ref[:, block] = lax.dot_general(
                picked, weight_ref[...], TN, preferred_element_type=F32
            ).astype(BF16)


def sum_kernel(got_ref, out_ref):
    rows, sources = out_ref.shape[0], got_ref.shape[0]
    pick = ones_where((iota((rows, sources), 0) & 7) == (iota((rows, sources), 1) & 7))
    out_ref[...] = jnp.dot(pick, got_ref[...], preferred_element_type=F32).astype(BF16)


def final_kernel(got_ref, out_ref):
    experts = out_ref.shape[0]
    sources, block = got_ref.shape
    row, col = iota((experts, sources), 0), iota((experts, sources), 1)
    for piece in range(4):
        pick = ones_where((col & 15) == ((piece >> 1) * 8 + row * 2 + (piece & 1)))
        out_ref[:, piece * block : (piece + 1) * block] = jnp.dot(
            pick, got_ref[...], preferred_element_type=F32
        )


def call(kernel, name, out_shape, *args, cost=None):
    return pl.pallas_call(
        kernel,
        in_specs=[
            pl.BlockSpec(memory_space=pltpu.SMEM if a.shape == (1,) else pltpu.VMEM) for a in args
        ],
        out_shape=out_shape,
        compiler_params=BIG,
        cost_estimate=cost,
        name=name,
    )(*args)


def body(activations, out_grad, router_weight, expert_ids, saved_output):
    experts, width = router_weight.shape
    tokens = activations.shape[0]
    planes = lax.axis_size("pairs") * lax.axis_size("side")
    rows = experts * saved_output.shape[2]
    core = lax.axis_index("core").astype(jnp.int32).reshape(1)
    ids = expert_ids.T

    def swap(x):
        return lax.ppermute(x, "core", [(0, 1), (1, 0)])

    packed = pack(saved_output.reshape(rows, width), router_weight)
    got = lax.all_to_all(packed, ("core", "chip"), split_axis=0, concat_axis=0, tiled=True)
    other, other_rest = [swap(x) for x in halves_for_other(core, activations, out_grad)]
    other_ids = swap(ids)
    mine, own, rest = gate_dots(
        core, ids, other_ids, other, got, other_rest, activations, out_grad
    )
    score_grad, part = call(
        score_kernel,
        "scores",
        (
            jax.ShapeDtypeStruct((2, tokens), F32),
            jax.ShapeDtypeStruct((rows, width // 4), BF16),
        ),
        core,
        mine,
        swap(mine),
        ids,
        other_ids,
        own,
        other,
        rest,
    )
    part = lax.all_to_all(part, ("side", "chip"), split_axis=0, concat_axis=0, tiled=True)
    summed = call(
        sum_kernel,
        "sum_chips",
        jax.ShapeDtypeStruct((planes * 2 * experts, width // 4), BF16),
        part,
    )
    got, summed = lax.optimization_barrier((got, summed))
    weight = got[:, width:]
    input_grad = call(
        input_kernel,
        "input_grads",
        jax.ShapeDtypeStruct((tokens, width), BF16),
        core,
        ids,
        score_grad,
        weight,
        swap(weight),
        cost=pl.CostEstimate(
            flops=2 * tokens * rows * width, bytes_accessed=4 * tokens * width, transcendentals=0
        ),
    )
    summed = lax.all_to_all(summed, ("pairs", "side"), split_axis=0, concat_axis=0, tiled=True)
    router_grad = call(
        final_kernel, "sum_batches", jax.ShapeDtypeStruct((experts, width), F32), summed
    )
    return input_grad, score_grad.T, router_grad


def solution(mesh):
    dp, owners = mesh.shape["dp"], mesh.shape["expert"]
    devices = mesh.devices.reshape(dp // 2, 2, owners // 2, 2)
    mesh = Mesh(devices, ("pairs", "side", "chip", "core"))
    tokens = P(("pairs", "side", "chip", "core"), None)
    in_specs = (
        tokens,
        tokens,
        P(("chip", "core"), None),
        tokens,
        P(("pairs", "side"), ("chip", "core"), None, None),
    )
    out_specs = (tokens, tokens, P(("chip", "core"), None))
    return jax.shard_map(body, mesh=mesh, in_specs=in_specs, out_specs=out_specs, check_vma=False)
```

```python
import jax
import jax.numpy as jnp
from jax import lax
from jax.experimental import pallas as pl
from jax.experimental.pallas import tpu as pltpu
from jax.sharding import Mesh, PartitionSpec as P

route_scale = 2.5
BF16, F32 = jnp.bfloat16, jnp.float32
NT = (((1,), (1,)), ((), ()))
TN = (((0,), (0,)), ((), ()))
CHIP, PLANE = 10, 10
BIG = pltpu.CompilerParams(vmem_limit_bytes=40 * 1024 * 1024)


def iota(shape, dim):
    return lax.broadcasted_iota(jnp.int32, shape, dim)


def chip_at(place, chips):
    return (place + CHIP) & (chips - 1)


def ones_where(mask):
    return jnp.where(mask, 1.0, 0.0).astype(BF16)


def pack_kernel(saved_hbm, weight_hbm, out_hbm, saved_ref, weight_ref, out_ref, in_sem, out_sem):
    rows, width = saved_ref.shape
    half, quarter, per_core = width // 2, width // 4, rows // 2
    halves = [slice(k * half, (k + 1) * half) for k in range(2)]
    copies = [
        pltpu.make_async_copy(saved_hbm.at[:, block], saved_ref.at[:, block], in_sem.at[k])
        for k, block in enumerate(halves)
    ]
    copies.append(pltpu.make_async_copy(weight_hbm, weight_ref, in_sem.at[2]))
    for i in (0, 2, 1):
        copies[i].start()
    row, col = iota((rows, rows), 0), iota((rows, rows), 1)
    local = row & (per_core - 1)
    chip = chip_at(local >> 3, per_core // 8)
    source = ((local >> 1) & 3) * (rows // 4) + chip * 4 + (local & 1)
    pick = ones_where(col == source + jnp.where(row < per_core, 0, 2))
    row, col = iota((per_core, 8), 0), iota((per_core, 8), 1)
    pick_weight = ones_where(col == ((row >> 1) & 3) + (row & 1) * 4)
    copies[2].wait()
    sent = []
    for k, block in enumerate(halves):
        mine = slice((1 - k) * per_core, (2 - k) * per_core)
        parts = [
            weight_ref[:, k * half + m * quarter : k * half + (m + 1) * quarter] for m in range(2)
        ]
        out_ref[mine, width:] = jnp.dot(
            pick_weight, jnp.concatenate(parts, axis=0), preferred_element_type=F32
        ).astype(BF16)
        copies[k].wait()
        out = jnp.dot(pick, saved_ref[:, block], preferred_element_type=F32).astype(BF16)
        for core in range(2):
            out_ref[mine, halves[core]] = out[core * per_core : (core + 1) * per_core]
        sent.append(pltpu.make_async_copy(out_ref.at[mine], out_hbm.at[mine], out_sem.at[k]))
        sent[k].start()
    for copy in sent:
        copy.wait()


def pack(saved, weight):
    rows, width = saved.shape
    packed = (rows, width + width // 4)
    return pl.pallas_call(
        pack_kernel,
        in_specs=[pl.BlockSpec(memory_space=pltpu.HBM)] * 2,
        out_specs=pl.BlockSpec(memory_space=pltpu.HBM),
        out_shape=pltpu.HBM(packed, BF16),
        scratch_shapes=[
            pltpu.VMEM((rows, width), BF16),
            pltpu.VMEM(weight.shape, BF16),
            pltpu.VMEM(packed, BF16),
            pltpu.SemaphoreType.DMA((3,)),
            pltpu.SemaphoreType.DMA((2,)),
        ],
        compiler_params=BIG,
        name="pack_rows",
    )(in_hbm(saved), in_hbm(weight))


def in_hbm(array):
    return pltpu.with_memory_space_constraint(array, pltpu.HBM)


def half_copies(pieces, sems):
    copies = []
    for i, (array, half, out_ref) in enumerate(pieces):
        width = out_ref.shape[1]
        block = pl.ds(pl.multiple_of(half * width, 128), width)
        copies.append(pltpu.make_async_copy(array.at[:, block], out_ref, sems.at[i]))
    return copies


def halves_kernel(core_ref, act_hbm, grad_hbm, out_ref, rest_ref, sem):
    tokens = act_hbm.shape[0]
    mine, theirs = core_ref[0], 1 - core_ref[0]
    copies = half_copies(
        [
            (act_hbm, theirs, out_ref.at[pl.ds(0, tokens)]),
            (grad_hbm, theirs, out_ref.at[pl.ds(tokens, tokens)]),
            (act_hbm, mine, rest_ref),
        ],
        sem,
    )
    for copy in copies:
        copy.start()
    for copy in copies:
        copy.wait()


def halves_for_other(core, act, grad):
    tokens, width = act.shape
    return pl.pallas_call(
        halves_kernel,
        in_specs=[pl.BlockSpec(memory_space=pltpu.SMEM)]
        + [pl.BlockSpec(memory_space=pltpu.HBM)] * 2,
        out_shape=(
            jax.ShapeDtypeStruct((2 * tokens, width // 2), BF16),
            jax.ShapeDtypeStruct((tokens, width // 2), BF16),
        ),
        scratch_shapes=[pltpu.SemaphoreType.DMA((3,))],
        compiler_params=BIG,
        name="halves_for_other",
    )(core, in_hbm(act), in_hbm(grad))


def named_rows(ids, rows):
    row = iota((rows, ids.shape[1]), 0)
    chip = chip_at(row >> 3, rows // 16)
    expert = chip * 8 + (row < rows // 2) * 4 + ((row >> 1) & 3)
    return [expert == ids[k : k + 1, :] for k in range(2)]


def odd_rows(rows, tokens):
    return (iota((rows, tokens), 0) & 1) == 1


def dots_kernel(
    core_ref,
    ids_ref,
    other_ids_ref,
    other_ref,
    got_ref,
    other_rest_hbm,
    act_hbm,
    grad_hbm,
    out_ref,
    own_ref,
    rest_ref,
    sem,
):
    rows = got_ref.shape[0]
    tokens, half = own_ref.shape[0] // 2, own_ref.shape[1]
    quarter = half // 2
    core = core_ref[0]
    low, high = pl.ds(0, tokens), pl.ds(tokens, tokens)
    copies = half_copies(
        [
            (act_hbm, core, own_ref.at[low]),
            (grad_hbm, core, own_ref.at[high]),
            (act_hbm, 1 - core, rest_ref.at[low]),
            (other_rest_hbm, 0, rest_ref.at[high]),
        ],
        sem,
    )
    for copy in copies:
        copy.start()
    odd = odd_rows(rows, tokens)
    before = ones_where(iota((tokens, tokens), 0) < iota((tokens, tokens), 1))
    for owner, ids, halves_ref in (
        (1 - core, other_ids_ref[...], other_ref),
        (core, ids_ref[...], own_ref),
    ):
        if halves_ref is own_ref:
            for copy in copies[:2]:
                copy.wait()
        saved = got_ref[:, pl.ds(pl.multiple_of(owner * half, 128), half)]
        dots = lax.dot_general(
            saved, halves_ref[tokens:, :], NT, preferred_element_type=F32
        )
        named = named_rows(ids, rows)
        earlier = jnp.dot(ones_where(named[0] | named[1]), before, preferred_element_type=F32)
        dots = jnp.where(earlier == jnp.where(odd, 1.0, 0.0), dots, 0.0)
        parts = [halves_ref[:tokens, :quarter], halves_ref[:tokens, quarter:]]
        logits = lax.dot_general(
            got_ref[:, 2 * half :],
            jnp.concatenate(parts, axis=0),
            NT,
            preferred_element_type=F32,
        )
        logits = jnp.where(odd, logits[:, tokens:], logits[:, :tokens])
        sums = [
            jnp.sum(jnp.where(named[k], values, 0.0), axis=0, keepdims=True)
            for values in (dots, logits)
            for k in range(2)
        ]
        sums.append(jnp.zeros((4, tokens), F32))
        out_ref[pl.ds(pl.multiple_of(owner * 8, 8), 8), :] = jnp.concatenate(sums, axis=0)
    for copy in copies[2:]:
        copy.wait()


def gate_dots(core, ids, other_ids, other, got, other_rest, act, grad):
    tokens = act.shape[0]
    vmem, hbm = pl.BlockSpec(memory_space=pltpu.VMEM), pl.BlockSpec(memory_space=pltpu.HBM)
    return pl.pallas_call(
        dots_kernel,
        in_specs=[pl.BlockSpec(memory_space=pltpu.SMEM)] + [vmem] * 4 + [hbm] * 3,
        out_shape=(
            jax.ShapeDtypeStruct((16, tokens), F32),
            jax.ShapeDtypeStruct(other.shape, BF16),
            jax.ShapeDtypeStruct(other.shape, BF16),
        ),
        scratch_shapes=[pltpu.SemaphoreType.DMA((4,))],
        compiler_params=BIG,
        name="gate_dots",
    )(core, ids, other_ids, other, got, in_hbm(other_rest), in_hbm(act), in_hbm(grad))


def score_kernel(
    core_ref, mine_ref, theirs_ref, ids_ref, other_ids_ref, own_ref, other_ref, rest_ref, *outs
):
    score_grad_ref, part_ref = outs
    rows, quarter = part_ref.shape[0] // 2, part_ref.shape[1]
    tokens = ids_ref.shape[1]
    core = core_ref[0]
    odd = odd_rows(rows, tokens)
    row = iota((rows, tokens), 0)
    expert = chip_at(row >> 3, rows // 8) * 8 + core * 4 + ((row >> 1) & 3)
    left = []
    for owner, ids in ((core, ids_ref[...]), (1 - core, other_ids_ref[...])):
        block = pl.ds(pl.multiple_of(owner * 8, 8), 8)
        sums = mine_ref[block, :] + theirs_ref[block, :]
        gate = [sums[k : k + 1, :] for k in range(2)]
        score = [jax.nn.sigmoid(sums[2 + k : 3 + k, :]) for k in range(2)]
        total = score[0] + score[1]
        mean_term = (score[0] * gate[0] + score[1] * gate[1]) / total
        dense = jnp.zeros((rows, tokens), F32)
        for k in range(2):
            grad = route_scale / total * (gate[k] - mean_term) * score[k] * (1.0 - score[k])
            if not left:
                score_grad_ref[k : k + 1, :] = grad
            dense = jnp.where(expert == ids[k : k + 1, :], grad, dense)
        left += [jnp.where(odd, 0.0, dense).astype(BF16), jnp.where(odd, dense, 0.0).astype(BF16)]
    left = jnp.concatenate(left, axis=1)
    for side, acts in (
        (core, (own_ref[:tokens, :], other_ref[:tokens, :])),
        (1 - core, (rest_ref[:tokens, :], rest_ref[tokens:, :])),
    ):
        right = [act[:, h * quarter : (h + 1) * quarter] for act in acts for h in range(2)]
        part_ref[pl.ds(pl.multiple_of(side * rows, 16), rows), :] = jnp.dot(
            left, jnp.concatenate(right, axis=0), preferred_element_type=F32
        ).astype(BF16)


def input_kernel(core_ref, ids_ref, score_grad_ref, own_ref, other_ref, out_ref):
    rows, quarter = own_ref.shape
    tokens = out_ref.shape[0]
    odd = odd_rows(rows, tokens)
    named = named_rows(ids_ref[...], rows)
    dense = jnp.zeros((rows, tokens), F32)
    for k in range(2):
        dense = jnp.where(named[k], score_grad_ref[k : k + 1, :], dense)
    for m in range(2):
        picked = jnp.where(odd == (m == 1), dense, 0.0).astype(BF16)
        for core, weight_ref in ((core_ref[0], own_ref), (1 - core_ref[0], other_ref)):
            block = pl.ds(pl.multiple_of((core * 2 + m) * quarter, 128), quarter)
            out_ref[:, block] = lax.dot_general(
                picked, weight_ref[...], TN, preferred_element_type=F32
            ).astype(BF16)


def sum_kernel(got_ref, out_ref):
    rows, sources = out_ref.shape[0], got_ref.shape[0]
    pick = ones_where((iota((rows, sources), 0) & 7) == (iota((rows, sources), 1) & 7))
    out_ref[...] = jnp.dot(pick, got_ref[...], preferred_element_type=F32).astype(BF16)


def final_kernel(got_ref, out_ref):
    experts = out_ref.shape[0]
    sources, block = got_ref.shape
    row, col = iota((experts, sources), 0), iota((experts, sources), 1)
    for piece in range(4):
        pick = ones_where((col & 15) == ((piece >> 1) * 8 + row * 2 + (piece & 1)))
        out_ref[:, piece * block : (piece + 1) * block] = jnp.dot(
            pick, got_ref[...], preferred_element_type=F32
        )


def call(kernel, name, out_shape, *args, cost=None):
    return pl.pallas_call(
        kernel,
        in_specs=[
            pl.BlockSpec(memory_space=pltpu.SMEM if a.shape == (1,) else pltpu.VMEM) for a in args
        ],
        out_shape=out_shape,
        compiler_params=BIG,
        cost_estimate=cost,
        name=name,
    )(*args)


def exchange(x, axes, order):
    return lax.all_to_all(
        x, axes, split_axis=0, concat_axis=0, tiled=True, axis_index_groups=[order]
    )


def body(activations, out_grad, router_weight, expert_ids, saved_output):
    experts, width = router_weight.shape
    tokens = activations.shape[0]
    planes = lax.axis_size("pairs") * lax.axis_size("side")
    chips = lax.axis_size("chip")
    chip_order = [chip_at(i, chips) for i in range(chips)]
    rows = experts * saved_output.shape[2]
    core = lax.axis_index("core").astype(jnp.int32).reshape(1)
    ids = expert_ids.T

    def swap(x):
        return lax.ppermute(x, "core", [(0, 1), (1, 0)])

    packed = pack(saved_output.reshape(rows, width), router_weight)
    order = [core * chips + chip for core in (1, 0) for chip in chip_order]
    got = exchange(packed, ("core", "chip"), order)
    other, other_rest = [swap(x) for x in halves_for_other(core, activations, out_grad)]
    other_ids = swap(ids)
    mine, own, rest = gate_dots(
        core, ids, other_ids, other, got, other_rest, activations, out_grad
    )
    score_grad, part = call(
        score_kernel,
        "scores",
        (
            jax.ShapeDtypeStruct((2, tokens), F32),
            jax.ShapeDtypeStruct((rows, width // 4), BF16),
        ),
        core,
        mine,
        swap(mine),
        ids,
        other_ids,
        own,
        other,
        rest,
    )
    order = [side * chips + chip for side in (0, 1) for chip in chip_order]
    part = exchange(part, ("side", "chip"), order)
    summed = call(
        sum_kernel,
        "sum_chips",
        jax.ShapeDtypeStruct((planes * 2 * experts, width // 4), BF16),
        part,
    )
    got, summed = lax.optimization_barrier((got, summed))
    weight = got[:, width:]
    input_grad = call(
        input_kernel,
        "input_grads",
        jax.ShapeDtypeStruct((tokens, width), BF16),
        core,
        ids,
        score_grad,
        weight,
        swap(weight),
        cost=pl.CostEstimate(
            flops=2 * tokens * rows * width, bytes_accessed=4 * tokens * width, transcendentals=0
        ),
    )
    summed = exchange(summed, ("pairs", "side"), [(i + PLANE) % planes for i in range(planes)])
    router_grad = call(
        final_kernel, "sum_batches", jax.ShapeDtypeStruct((experts, width), F32), summed
    )
    return input_grad, score_grad.T, router_grad


def solution(mesh):
    dp, owners = mesh.shape["dp"], mesh.shape["expert"]
    devices = mesh.devices.reshape(dp // 2, 2, owners // 2, 2)
    mesh = Mesh(devices, ("pairs", "side", "chip", "core"))
    tokens = P(("pairs", "side", "chip", "core"), None)
    in_specs = (
        tokens,
        tokens,
        P(("chip", "core"), None),
        tokens,
        P(("pairs", "side"), ("chip", "core"), None, None),
    )
    out_specs = (tokens, tokens, P(("chip", "core"), None))
    return jax.shard_map(body, mesh=mesh, in_specs=in_specs, out_specs=out_specs, check_vma=False)
```

```python
import jax
import jax.numpy as jnp
from jax import lax
from jax.experimental import pallas as pl
from jax.experimental.pallas import tpu as pltpu
from jax.sharding import Mesh, PartitionSpec as P

route_scale = 2.5
BF16, F32 = jnp.bfloat16, jnp.float32
NT = (((1,), (1,)), ((), ()))
TN = (((0,), (0,)), ((), ()))
CHIP, PLANE = 10, 10
BIG = pltpu.CompilerParams(vmem_limit_bytes=40 * 1024 * 1024)


def iota(shape, dim):
    return lax.broadcasted_iota(jnp.int32, shape, dim)


def chip_at(place, chips):
    return (place + CHIP) & (chips - 1)


def ones_where(mask):
    return jnp.where(mask, 1.0, 0.0).astype(BF16)


def pack_kernel(saved_hbm, weight_hbm, out_hbm, saved_ref, weight_ref, out_ref, in_sem, out_sem):
    rows, width = saved_ref.shape
    half, quarter, per_core = width // 2, width // 4, rows // 2
    halves = [slice(k * half, (k + 1) * half) for k in range(2)]
    copies = [
        pltpu.make_async_copy(saved_hbm.at[:, block], saved_ref.at[:, block], in_sem.at[k])
        for k, block in enumerate(halves)
    ]
    copies.append(pltpu.make_async_copy(weight_hbm, weight_ref, in_sem.at[2]))
    for i in (0, 2, 1):
        copies[i].start()
    row, col = iota((rows, rows), 0), iota((rows, rows), 1)
    local = row & (per_core - 1)
    chip = chip_at(local >> 3, per_core // 8)
    source = ((local >> 1) & 3) * (rows // 4) + chip * 4 + (local & 1)
    pick = ones_where(col == source + jnp.where(row < per_core, 0, 2))
    row, col = iota((per_core, 8), 0), iota((per_core, 8), 1)
    pick_weight = ones_where(col == ((row >> 1) & 3) + (row & 1) * 4)
    copies[2].wait()
    sent = []
    for k, block in enumerate(halves):
        mine = slice((1 - k) * per_core, (2 - k) * per_core)
        parts = [
            weight_ref[:, k * half + m * quarter : k * half + (m + 1) * quarter] for m in range(2)
        ]
        out_ref[mine, width:] = jnp.dot(
            pick_weight, jnp.concatenate(parts, axis=0), preferred_element_type=F32
        ).astype(BF16)
        copies[k].wait()
        for core in range(2):
            out_ref[mine, halves[core]] = jnp.dot(
                pick[core * per_core : (core + 1) * per_core],
                saved_ref[:, block],
                preferred_element_type=F32,
            ).astype(BF16)
            columns = slice(0, half) if core == 0 else slice(half, width + quarter)
            sent.append(
                pltpu.make_async_copy(
                    out_ref.at[mine, columns], out_hbm.at[mine, columns], out_sem.at[len(sent)]
                )
            )
            sent[-1].start()
    for copy in sent:
        copy.wait()


def pack(saved, weight):
    rows, width = saved.shape
    packed = (rows, width + width // 4)
    return pl.pallas_call(
        pack_kernel,
        in_specs=[pl.BlockSpec(memory_space=pltpu.HBM)] * 2,
        out_specs=pl.BlockSpec(memory_space=pltpu.HBM),
        out_shape=pltpu.HBM(packed, BF16),
        scratch_shapes=[
            pltpu.VMEM((rows, width), BF16),
            pltpu.VMEM(weight.shape, BF16),
            pltpu.VMEM(packed, BF16),
            pltpu.SemaphoreType.DMA((3,)),
            pltpu.SemaphoreType.DMA((4,)),
        ],
        compiler_params=BIG,
        name="pack_rows",
    )(in_hbm(saved), in_hbm(weight))


def in_hbm(array):
    return pltpu.with_memory_space_constraint(array, pltpu.HBM)


def half_copies(pieces, sems):
    copies = []
    for i, (array, half, out_ref) in enumerate(pieces):
        width = out_ref.shape[1]
        block = pl.ds(pl.multiple_of(half * width, 128), width)
        copies.append(pltpu.make_async_copy(array.at[:, block], out_ref, sems.at[i]))
    return copies


def halves_kernel(core_ref, act_hbm, grad_hbm, out_ref, rest_ref, own_rest_ref, sem):
    tokens = act_hbm.shape[0]
    mine, theirs = core_ref[0], 1 - core_ref[0]
    copies = half_copies(
        [
            (act_hbm, theirs, out_ref.at[pl.ds(0, tokens)]),
            (grad_hbm, theirs, out_ref.at[pl.ds(tokens, tokens)]),
            (act_hbm, mine, rest_ref),
            (act_hbm, theirs, own_rest_ref),
        ],
        sem,
    )
    for copy in copies:
        copy.start()
    for copy in copies:
        copy.wait()


def halves_for_other(core, act, grad):
    tokens, width = act.shape
    return pl.pallas_call(
        halves_kernel,
        in_specs=[pl.BlockSpec(memory_space=pltpu.SMEM)]
        + [pl.BlockSpec(memory_space=pltpu.HBM)] * 2,
        out_shape=(
            jax.ShapeDtypeStruct((2 * tokens, width // 2), BF16),
            jax.ShapeDtypeStruct((tokens, width // 2), BF16),
            pltpu.HBM((tokens, width // 2), BF16),
        ),
        scratch_shapes=[pltpu.SemaphoreType.DMA((4,))],
        compiler_params=BIG,
        name="halves_for_other",
    )(core, in_hbm(act), in_hbm(grad))


def named_rows(ids, rows):
    row = iota((rows, ids.shape[1]), 0)
    chip = chip_at(row >> 3, rows // 16)
    expert = chip * 8 + (row < rows // 2) * 4 + ((row >> 1) & 3)
    return [expert == ids[k : k + 1, :] for k in range(2)]


def odd_rows(rows, tokens):
    return (iota((rows, tokens), 0) & 1) == 1


def dots_kernel(
    core_ref,
    ids_ref,
    other_ids_ref,
    other_ref,
    got_ref,
    act_hbm,
    grad_hbm,
    out_ref,
    own_ref,
    sem,
):
    rows = got_ref.shape[0]
    tokens, half = own_ref.shape[0] // 2, own_ref.shape[1]
    quarter = half // 2
    core = core_ref[0]
    low, high = pl.ds(0, tokens), pl.ds(tokens, tokens)
    copies = half_copies(
        [
            (act_hbm, core, own_ref.at[low]),
            (grad_hbm, core, own_ref.at[high]),
        ],
        sem,
    )
    for copy in copies:
        copy.start()
    odd = odd_rows(rows, tokens)
    before = ones_where(iota((tokens, tokens), 0) < iota((tokens, tokens), 1))
    for owner, ids, halves_ref in (
        (1 - core, other_ids_ref[...], other_ref),
        (core, ids_ref[...], own_ref),
    ):
        if halves_ref is own_ref:
            for copy in copies:
                copy.wait()
        saved = got_ref[:, pl.ds(pl.multiple_of(owner * half, 128), half)]
        dots = lax.dot_general(
            saved, halves_ref[tokens:, :], NT, preferred_element_type=F32
        )
        named = named_rows(ids, rows)
        earlier = jnp.dot(ones_where(named[0] | named[1]), before, preferred_element_type=F32)
        dots = jnp.where(earlier == jnp.where(odd, 1.0, 0.0), dots, 0.0)
        parts = [halves_ref[:tokens, :quarter], halves_ref[:tokens, quarter:]]
        logits = lax.dot_general(
            got_ref[:, 2 * half :],
            jnp.concatenate(parts, axis=0),
            NT,
            preferred_element_type=F32,
        )
        logits = jnp.where(odd, logits[:, tokens:], logits[:, :tokens])
        sums = [
            jnp.sum(jnp.where(named[k], values, 0.0), axis=0, keepdims=True)
            for values in (dots, logits)
            for k in range(2)
        ]
        sums.append(jnp.zeros((4, tokens), F32))
        out_ref[pl.ds(pl.multiple_of(owner * 8, 8), 8), :] = jnp.concatenate(sums, axis=0)


def stage_kernel(own_hbm, other_hbm, out_ref, sem):
    tokens = own_hbm.shape[0]
    copies = [
        pltpu.make_async_copy(array, out_ref.at[pl.ds(i * tokens, tokens)], sem.at[i])
        for i, array in enumerate((own_hbm, other_hbm))
    ]
    for copy in copies:
        copy.start()
    for copy in copies:
        copy.wait()


def stage(own, other):
    return pl.pallas_call(
        stage_kernel,
        in_specs=[pl.BlockSpec(memory_space=pltpu.HBM)] * 2,
        out_shape=jax.ShapeDtypeStruct((2 * own.shape[0], own.shape[1]), BF16),
        scratch_shapes=[pltpu.SemaphoreType.DMA((2,))],
        compiler_params=BIG,
        name="stage",
    )(in_hbm(own), in_hbm(other))


def gate_dots(core, ids, other_ids, other, got, act, grad):
    tokens = act.shape[0]
    vmem, hbm = pl.BlockSpec(memory_space=pltpu.VMEM), pl.BlockSpec(memory_space=pltpu.HBM)
    return pl.pallas_call(
        dots_kernel,
        in_specs=[pl.BlockSpec(memory_space=pltpu.SMEM)] + [vmem] * 4 + [hbm] * 2,
        out_shape=(
            jax.ShapeDtypeStruct((16, tokens), F32),
            jax.ShapeDtypeStruct(other.shape, BF16),
        ),
        scratch_shapes=[pltpu.SemaphoreType.DMA((2,))],
        compiler_params=BIG,
        name="gate_dots",
    )(core, ids, other_ids, other, got, in_hbm(act), in_hbm(grad))


def score_kernel(
    core_ref, mine_ref, theirs_ref, ids_ref, other_ids_ref, own_ref, other_ref, rest_ref, *outs
):
    score_grad_ref, part_ref = outs
    rows, quarter = part_ref.shape[0] // 2, part_ref.shape[1]
    tokens = ids_ref.shape[1]
    core = core_ref[0]
    odd = odd_rows(rows, tokens)
    row = iota((rows, tokens), 0)
    expert = chip_at(row >> 3, rows // 8) * 8 + core * 4 + ((row >> 1) & 3)
    left = []
    for owner, ids in ((core, ids_ref[...]), (1 - core, other_ids_ref[...])):
        block = pl.ds(pl.multiple_of(owner * 8, 8), 8)
        sums = mine_ref[block, :] + theirs_ref[block, :]
        gate = [sums[k : k + 1, :] for k in range(2)]
        score = [jax.nn.sigmoid(sums[2 + k : 3 + k, :]) for k in range(2)]
        total = score[0] + score[1]
        mean_term = (score[0] * gate[0] + score[1] * gate[1]) / total
        dense = jnp.zeros((rows, tokens), F32)
        for k in range(2):
            grad = route_scale / total * (gate[k] - mean_term) * score[k] * (1.0 - score[k])
            if not left:
                score_grad_ref[k : k + 1, :] = grad
            dense = jnp.where(expert == ids[k : k + 1, :], grad, dense)
        left += [jnp.where(odd, 0.0, dense).astype(BF16), jnp.where(odd, dense, 0.0).astype(BF16)]
    left = jnp.concatenate(left, axis=1)
    for side, acts in (
        (core, (own_ref[:tokens, :], other_ref[:tokens, :])),
        (1 - core, (rest_ref[:tokens, :], rest_ref[tokens:, :])),
    ):
        right = [act[:, h * quarter : (h + 1) * quarter] for act in acts for h in range(2)]
        part_ref[pl.ds(pl.multiple_of((1 - side) * rows, 16), rows), :] = jnp.dot(
            left, jnp.concatenate(right, axis=0), preferred_element_type=F32
        ).astype(BF16)


def input_kernel(core_ref, ids_ref, score_grad_ref, own_ref, other_ref, out_ref):
    rows, quarter = own_ref.shape
    tokens = out_ref.shape[0]
    odd = odd_rows(rows, tokens)
    named = named_rows(ids_ref[...], rows)
    dense = jnp.zeros((rows, tokens), F32)
    for k in range(2):
        dense = jnp.where(named[k], score_grad_ref[k : k + 1, :], dense)
    for m in range(2):
        picked = jnp.where(odd == (m == 1), dense, 0.0).astype(BF16)
        for core, weight_ref in ((core_ref[0], own_ref), (1 - core_ref[0], other_ref)):
            block = pl.ds(pl.multiple_of((core * 2 + m) * quarter, 128), quarter)
            out_ref[:, block] = lax.dot_general(
                picked, weight_ref[...], TN, preferred_element_type=F32
            ).astype(BF16)


def sum_kernel(got_ref, out_ref):
    rows, sources = out_ref.shape[0], got_ref.shape[0]
    pick = ones_where((iota((rows, sources), 0) & 7) == (iota((rows, sources), 1) & 7))
    out_ref[...] = jnp.dot(pick, got_ref[...], preferred_element_type=F32).astype(BF16)


def final_kernel(got_ref, out_ref):
    experts = out_ref.shape[0]
    sources, block = got_ref.shape
    row, col = iota((experts, sources), 0), iota((experts, sources), 1)
    for piece in range(4):
        pick = ones_where((col & 15) == ((piece >> 1) * 8 + row * 2 + (piece & 1)))
        out_ref[:, piece * block : (piece + 1) * block] = jnp.dot(
            pick, got_ref[...], preferred_element_type=F32
        )


def call(kernel, name, out_shape, *args, cost=None):
    return pl.pallas_call(
        kernel,
        in_specs=[
            pl.BlockSpec(memory_space=pltpu.SMEM if a.shape == (1,) else pltpu.VMEM) for a in args
        ],
        out_shape=out_shape,
        compiler_params=BIG,
        cost_estimate=cost,
        name=name,
    )(*args)


def exchange(x, axes, order):
    return lax.all_to_all(
        x, axes, split_axis=0, concat_axis=0, tiled=True, axis_index_groups=[order]
    )


def body(activations, out_grad, router_weight, expert_ids, saved_output):
    experts, width = router_weight.shape
    tokens = activations.shape[0]
    planes = lax.axis_size("pairs") * lax.axis_size("side")
    chips = lax.axis_size("chip")
    chip_order = [chip_at(i, chips) for i in range(chips)]
    rows = experts * saved_output.shape[2]
    core = lax.axis_index("core").astype(jnp.int32).reshape(1)
    ids = expert_ids.T

    def swap(x):
        return lax.ppermute(x, "core", [(0, 1), (1, 0)])

    packed = pack(saved_output.reshape(rows, width), router_weight)
    order = [core * chips + chip for core in (1, 0) for chip in chip_order]
    got = exchange(packed, ("core", "chip"), order)
    other, other_rest, own_rest = halves_for_other(core, activations, out_grad)
    other, other_rest = swap(other), swap(other_rest)
    other_ids = swap(ids)
    mine, own = gate_dots(core, ids, other_ids, other, got, activations, out_grad)
    mine, own_rest, other_rest = lax.optimization_barrier((mine, own_rest, other_rest))
    theirs = swap(mine)
    rest = stage(own_rest, other_rest)
    score_grad, part = call(
        score_kernel,
        "scores",
        (
            jax.ShapeDtypeStruct((2, tokens), F32),
            jax.ShapeDtypeStruct((rows, width // 4), BF16),
        ),
        core,
        mine,
        theirs,
        ids,
        other_ids,
        own,
        other,
        rest,
    )
    order = [side * chips + chip for side in (1, 0) for chip in chip_order]
    part = exchange(part, ("side", "chip"), order)
    summed = call(
        sum_kernel,
        "sum_chips",
        jax.ShapeDtypeStruct((planes * 2 * experts, width // 4), BF16),
        part,
    )
    got, summed = lax.optimization_barrier((got, summed))
    weight = got[:, width:]
    input_grad = call(
        input_kernel,
        "input_grads",
        jax.ShapeDtypeStruct((tokens, width), BF16),
        core,
        ids,
        score_grad,
        weight,
        swap(weight),
        cost=pl.CostEstimate(
            flops=2 * tokens * rows * width, bytes_accessed=4 * tokens * width, transcendentals=0
        ),
    )
    summed = exchange(summed, ("pairs", "side"), [(i + PLANE) % planes for i in range(planes)])
    router_grad = call(
        final_kernel, "sum_batches", jax.ShapeDtypeStruct((experts, width), F32), summed
    )
    return input_grad, score_grad.T, router_grad


def solution(mesh):
    dp, owners = mesh.shape["dp"], mesh.shape["expert"]
    devices = mesh.devices.reshape(dp // 2, 2, owners // 2, 2)
    mesh = Mesh(devices, ("pairs", "side", "chip", "core"))
    tokens = P(("pairs", "side", "chip", "core"), None)
    in_specs = (
        tokens,
        tokens,
        P(("chip", "core"), None),
        tokens,
        P(("pairs", "side"), ("chip", "core"), None, None),
    )
    out_specs = (tokens, tokens, P(("chip", "core"), None))
    return jax.shard_map(body, mesh=mesh, in_specs=in_specs, out_specs=out_specs, check_vma=False)
```

```python
import jax
import jax.numpy as jnp
from jax import lax
from jax.experimental import pallas as pl
from jax.experimental.pallas import tpu as pltpu
from jax.sharding import Mesh, PartitionSpec as P

route_scale = 2.5
BF16, F32 = jnp.bfloat16, jnp.float32
NT = (((1,), (1,)), ((), ()))
TN = (((0,), (0,)), ((), ()))
CHIP, PLANE = 10, 10
BIG = pltpu.CompilerParams(vmem_limit_bytes=40 * 1024 * 1024)


def iota(shape, dim):
    return lax.broadcasted_iota(jnp.int32, shape, dim)


def chip_at(place, chips):
    return (place + CHIP) & (chips - 1)


def ones_where(mask):
    return jnp.where(mask, 1.0, 0.0).astype(BF16)


def pack_kernel(saved_hbm, weight_hbm, out_hbm, saved_ref, weight_ref, out_ref, in_sem, out_sem):
    rows, width = saved_ref.shape
    half, quarter, per_core = width // 2, width // 4, rows // 2
    halves = [slice(k * half, (k + 1) * half) for k in range(2)]
    copies = [
        pltpu.make_async_copy(saved_hbm.at[:, block], saved_ref.at[:, block], in_sem.at[k])
        for k, block in enumerate(halves)
    ]
    copies.append(pltpu.make_async_copy(weight_hbm, weight_ref, in_sem.at[2]))
    for i in (0, 2, 1):
        copies[i].start()
    row, col = iota((rows, rows), 0), iota((rows, rows), 1)
    local = row & (per_core - 1)
    chip = chip_at(local >> 3, per_core // 8)
    source = ((local >> 1) & 3) * (rows // 4) + chip * 4 + (local & 1)
    pick = ones_where(col == source + jnp.where(row < per_core, 0, 2))
    row, col = iota((per_core, 8), 0), iota((per_core, 8), 1)
    pick_weight = ones_where(col == ((row >> 1) & 3) + (row & 1) * 4)
    copies[2].wait()
    sent = []
    for k, block in enumerate(halves):
        mine = slice((1 - k) * per_core, (2 - k) * per_core)
        parts = [
            weight_ref[:, k * half + m * quarter : k * half + (m + 1) * quarter] for m in range(2)
        ]
        out_ref[mine, width:] = jnp.dot(
            pick_weight, jnp.concatenate(parts, axis=0), preferred_element_type=F32
        ).astype(BF16)
        copies[k].wait()
        for core in range(2):
            out_ref[mine, halves[core]] = jnp.dot(
                pick[core * per_core : (core + 1) * per_core],
                saved_ref[:, block],
                preferred_element_type=F32,
            ).astype(BF16)
            columns = slice(0, half) if core == 0 else slice(half, width + quarter)
            sent.append(
                pltpu.make_async_copy(
                    out_ref.at[mine, columns], out_hbm.at[mine, columns], out_sem.at[len(sent)]
                )
            )
            sent[-1].start()
    for copy in sent:
        copy.wait()


def pack(saved, weight):
    rows, width = saved.shape
    packed = (rows, width + width // 4)
    return pl.pallas_call(
        pack_kernel,
        in_specs=[pl.BlockSpec(memory_space=pltpu.HBM)] * 2,
        out_specs=pl.BlockSpec(memory_space=pltpu.HBM),
        out_shape=pltpu.HBM(packed, BF16),
        scratch_shapes=[
            pltpu.VMEM((rows, width), BF16),
            pltpu.VMEM(weight.shape, BF16),
            pltpu.VMEM(packed, BF16),
            pltpu.SemaphoreType.DMA((3,)),
            pltpu.SemaphoreType.DMA((4,)),
        ],
        compiler_params=BIG,
        name="pack_rows",
    )(in_hbm(saved), in_hbm(weight))


def in_hbm(array):
    return pltpu.with_memory_space_constraint(array, pltpu.HBM)


def half_copies(pieces, sems):
    copies = []
    for i, (array, half, out_ref) in enumerate(pieces):
        width = out_ref.shape[1]
        block = pl.ds(pl.multiple_of(half * width, 128), width)
        copies.append(pltpu.make_async_copy(array.at[:, block], out_ref, sems.at[i]))
    return copies


def halves_kernel(core_ref, act_hbm, grad_hbm, out_ref, rest_ref, own_rest_ref, sem):
    tokens = act_hbm.shape[0]
    mine, theirs = core_ref[0], 1 - core_ref[0]
    copies = half_copies(
        [
            (act_hbm, theirs, out_ref.at[pl.ds(0, tokens)]),
            (grad_hbm, theirs, out_ref.at[pl.ds(tokens, tokens)]),
            (act_hbm, mine, rest_ref),
            (act_hbm, theirs, own_rest_ref),
        ],
        sem,
    )
    for copy in copies:
        copy.start()
    for copy in copies:
        copy.wait()


def halves_for_other(core, act, grad):
    tokens, width = act.shape
    return pl.pallas_call(
        halves_kernel,
        in_specs=[pl.BlockSpec(memory_space=pltpu.SMEM)]
        + [pl.BlockSpec(memory_space=pltpu.HBM)] * 2,
        out_shape=(
            jax.ShapeDtypeStruct((2 * tokens, width // 2), BF16),
            jax.ShapeDtypeStruct((tokens, width // 2), BF16),
            pltpu.HBM((tokens, width // 2), BF16),
        ),
        scratch_shapes=[pltpu.SemaphoreType.DMA((4,))],
        compiler_params=BIG,
        name="halves_for_other",
    )(core, in_hbm(act), in_hbm(grad))


def named_rows(ids, rows):
    row = iota((rows, ids.shape[1]), 0)
    chip = chip_at(row >> 3, rows // 16)
    expert = chip * 8 + (row < rows // 2) * 4 + ((row >> 1) & 3)
    return [expert == ids[k : k + 1, :] for k in range(2)]


def odd_rows(rows, tokens):
    return (iota((rows, tokens), 0) & 1) == 1


def dots_kernel(
    core_ref,
    ids_ref,
    other_ids_ref,
    other_ref,
    got_ref,
    act_hbm,
    grad_hbm,
    out_ref,
    own_ref,
    sem,
):
    rows = got_ref.shape[0]
    tokens, half = own_ref.shape[0] // 2, own_ref.shape[1]
    quarter = half // 2
    core = core_ref[0]
    low, high = pl.ds(0, tokens), pl.ds(tokens, tokens)
    copies = half_copies(
        [
            (act_hbm, core, own_ref.at[low]),
            (grad_hbm, core, own_ref.at[high]),
        ],
        sem,
    )
    for copy in copies:
        copy.start()
    odd = odd_rows(rows, tokens)
    before = ones_where(iota((tokens, tokens), 0) < iota((tokens, tokens), 1))
    for owner, ids, halves_ref in (
        (1 - core, other_ids_ref[...], other_ref),
        (core, ids_ref[...], own_ref),
    ):
        if halves_ref is own_ref:
            for copy in copies:
                copy.wait()
        saved = got_ref[:, pl.ds(pl.multiple_of(owner * half, 128), half)]
        dots = lax.dot_general(
            saved, halves_ref[tokens:, :], NT, preferred_element_type=F32
        )
        named = named_rows(ids, rows)
        earlier = jnp.dot(ones_where(named[0] | named[1]), before, preferred_element_type=F32)
        dots = jnp.where(earlier == jnp.where(odd, 1.0, 0.0), dots, 0.0)
        parts = [halves_ref[:tokens, :quarter], halves_ref[:tokens, quarter:]]
        logits = lax.dot_general(
            got_ref[:, 2 * half :],
            jnp.concatenate(parts, axis=0),
            NT,
            preferred_element_type=F32,
        )
        logits = jnp.where(odd, logits[:, tokens:], logits[:, :tokens])
        sums = [
            jnp.sum(jnp.where(named[k], values, 0.0), axis=0, keepdims=True)
            for values in (dots, logits)
            for k in range(2)
        ]
        sums.append(jnp.zeros((4, tokens), F32))
        out_ref[pl.ds(pl.multiple_of(owner * 8, 8), 8), :] = jnp.concatenate(sums, axis=0)


def stage_kernel(own_hbm, other_hbm, out_ref, sem):
    tokens = own_hbm.shape[0]
    copies = [
        pltpu.make_async_copy(array, out_ref.at[pl.ds(i * tokens, tokens)], sem.at[i])
        for i, array in enumerate((own_hbm, other_hbm))
    ]
    for copy in copies:
        copy.start()
    for copy in copies:
        copy.wait()


def stage(own, other):
    return pl.pallas_call(
        stage_kernel,
        in_specs=[pl.BlockSpec(memory_space=pltpu.HBM)] * 2,
        out_shape=jax.ShapeDtypeStruct((2 * own.shape[0], own.shape[1]), BF16),
        scratch_shapes=[pltpu.SemaphoreType.DMA((2,))],
        compiler_params=BIG,
        name="stage",
    )(in_hbm(own), in_hbm(other))


def gate_dots(core, ids, other_ids, other, got, act, grad):
    tokens = act.shape[0]
    vmem, hbm = pl.BlockSpec(memory_space=pltpu.VMEM), pl.BlockSpec(memory_space=pltpu.HBM)
    return pl.pallas_call(
        dots_kernel,
        in_specs=[pl.BlockSpec(memory_space=pltpu.SMEM)] + [vmem] * 4 + [hbm] * 2,
        out_shape=(
            jax.ShapeDtypeStruct((16, tokens), F32),
            jax.ShapeDtypeStruct(other.shape, BF16),
        ),
        scratch_shapes=[pltpu.SemaphoreType.DMA((2,))],
        compiler_params=BIG,
        name="gate_dots",
    )(core, ids, other_ids, other, got, in_hbm(act), in_hbm(grad))


def score_kernel(
    core_ref, mine_ref, theirs_ref, ids_ref, other_ids_ref, own_ref, other_ref, rest_ref, *outs
):
    score_grad_ref, part_ref = outs
    rows, quarter = part_ref.shape[0] // 2, part_ref.shape[1]
    tokens = ids_ref.shape[1]
    core = core_ref[0]
    odd = odd_rows(rows, tokens)
    row = iota((rows, tokens), 0)
    expert = chip_at(row >> 3, rows // 8) * 8 + core * 4 + ((row >> 1) & 3)
    left = []
    for owner, ids in ((core, ids_ref[...]), (1 - core, other_ids_ref[...])):
        block = pl.ds(pl.multiple_of(owner * 8, 8), 8)
        sums = mine_ref[block, :] + theirs_ref[block, :]
        gate = [sums[k : k + 1, :] for k in range(2)]
        score = [jax.nn.sigmoid(sums[2 + k : 3 + k, :]) for k in range(2)]
        total = score[0] + score[1]
        mean_term = (score[0] * gate[0] + score[1] * gate[1]) / total
        dense = jnp.zeros((rows, tokens), F32)
        for k in range(2):
            grad = route_scale / total * (gate[k] - mean_term) * score[k] * (1.0 - score[k])
            if not left:
                score_grad_ref[k : k + 1, :] = grad
            dense = jnp.where(expert == ids[k : k + 1, :], grad, dense)
        left += [jnp.where(odd, 0.0, dense).astype(BF16), jnp.where(odd, dense, 0.0).astype(BF16)]
    left = jnp.concatenate(left, axis=1)
    for side, acts in (
        (core, (own_ref[:tokens, :], other_ref[:tokens, :])),
        (1 - core, (rest_ref[:tokens, :], rest_ref[tokens:, :])),
    ):
        right = [act[:, h * quarter : (h + 1) * quarter] for act in acts for h in range(2)]
        part_ref[pl.ds(pl.multiple_of((1 - side) * rows, 16), rows), :] = jnp.dot(
            left, jnp.concatenate(right, axis=0), preferred_element_type=F32
        ).astype(BF16)


def input_kernel(core_ref, ids_ref, score_grad_ref, own_ref, other_ref, out_ref):
    rows, quarter = own_ref.shape
    tokens = out_ref.shape[0]
    odd = odd_rows(rows, tokens)
    named = named_rows(ids_ref[...], rows)
    dense = jnp.zeros((rows, tokens), F32)
    for k in range(2):
        dense = jnp.where(named[k], score_grad_ref[k : k + 1, :], dense)
    for m in range(2):
        picked = jnp.where(odd == (m == 1), dense, 0.0).astype(BF16)
        for core, weight_ref in ((core_ref[0], own_ref), (1 - core_ref[0], other_ref)):
            block = pl.ds(pl.multiple_of((core * 2 + m) * quarter, 128), quarter)
            out_ref[:, block] = lax.dot_general(
                picked, weight_ref[...], TN, preferred_element_type=F32
            ).astype(BF16)


def sum_kernel(got_ref, out_ref):
    rows, sources = out_ref.shape[0], got_ref.shape[0]
    pick = ones_where((iota((16, sources), 0) & 7) == (iota((16, sources), 1) & 7))
    total = jnp.dot(pick, got_ref[...], preferred_element_type=F32).astype(BF16)
    for start in range(0, rows, 16):
        out_ref[start : start + 16, :] = total


def final_kernel(got_ref, out_ref):
    experts = out_ref.shape[0]
    sources, block = got_ref.shape
    row, col = iota((4 * experts, sources), 0), iota((4 * experts, sources), 1)
    want = (row >> 3) * 8 + (row & 3) * 2 + ((row >> 2) & 1)
    total = jnp.dot(ones_where((col & 15) == want), got_ref[...], preferred_element_type=F32)
    for piece in range(4):
        out_ref[:, piece * block : (piece + 1) * block] = total[
            piece * experts : (piece + 1) * experts
        ]


def call(kernel, name, out_shape, *args, cost=None):
    return pl.pallas_call(
        kernel,
        in_specs=[
            pl.BlockSpec(memory_space=pltpu.SMEM if a.shape == (1,) else pltpu.VMEM) for a in args
        ],
        out_shape=out_shape,
        compiler_params=BIG,
        cost_estimate=cost,
        name=name,
    )(*args)


def exchange(x, axes, order):
    return lax.all_to_all(
        x, axes, split_axis=0, concat_axis=0, tiled=True, axis_index_groups=[order]
    )


def body(activations, out_grad, router_weight, expert_ids, saved_output):
    experts, width = router_weight.shape
    tokens = activations.shape[0]
    planes = lax.axis_size("pairs") * lax.axis_size("side")
    chips = lax.axis_size("chip")
    chip_order = [chip_at(i, chips) for i in range(chips)]
    rows = experts * saved_output.shape[2]
    core = lax.axis_index("core").astype(jnp.int32).reshape(1)
    ids = expert_ids.T

    def swap(x):
        return lax.ppermute(x, "core", [(0, 1), (1, 0)])

    packed = pack(saved_output.reshape(rows, width), router_weight)
    order = [core * chips + chip for core in (1, 0) for chip in chip_order]
    got = exchange(packed, ("core", "chip"), order)
    other, other_rest, own_rest = halves_for_other(core, activations, out_grad)
    other, other_rest = swap(other), swap(other_rest)
    other_ids = swap(ids)
    mine, own = gate_dots(core, ids, other_ids, other, got, activations, out_grad)
    mine, own_rest, other_rest = lax.optimization_barrier((mine, own_rest, other_rest))
    theirs = swap(mine)
    rest = stage(own_rest, other_rest)
    score_grad, part = call(
        score_kernel,
        "scores",
        (
            jax.ShapeDtypeStruct((2, tokens), F32),
            jax.ShapeDtypeStruct((rows, width // 4), BF16),
        ),
        core,
        mine,
        theirs,
        ids,
        other_ids,
        own,
        other,
        rest,
    )
    order = [side * chips + chip for side in (1, 0) for chip in chip_order]
    part = exchange(part, ("side", "chip"), order)
    summed = call(
        sum_kernel,
        "sum_chips",
        jax.ShapeDtypeStruct((planes * 2 * experts, width // 4), BF16),
        part,
    )
    got, summed = lax.optimization_barrier((got, summed))
    weight = got[:, width:]
    input_grad = call(
        input_kernel,
        "input_grads",
        jax.ShapeDtypeStruct((tokens, width), BF16),
        core,
        ids,
        score_grad,
        weight,
        swap(weight),
        cost=pl.CostEstimate(
            flops=2 * tokens * rows * width, bytes_accessed=4 * tokens * width, transcendentals=0
        ),
    )
    summed = exchange(summed, ("pairs", "side"), [(i + PLANE) % planes for i in range(planes)])
    router_grad = call(
        final_kernel, "sum_batches", jax.ShapeDtypeStruct((experts, width), F32), summed
    )
    return input_grad, score_grad.T, router_grad


def solution(mesh):
    dp, owners = mesh.shape["dp"], mesh.shape["expert"]
    devices = mesh.devices.reshape(dp // 2, 2, owners // 2, 2)
    mesh = Mesh(devices, ("pairs", "side", "chip", "core"))
    tokens = P(("pairs", "side", "chip", "core"), None)
    in_specs = (
        tokens,
        tokens,
        P(("chip", "core"), None),
        tokens,
        P(("pairs", "side"), ("chip", "core"), None, None),
    )
    out_specs = (tokens, tokens, P(("chip", "core"), None))
    return jax.shard_map(body, mesh=mesh, in_specs=in_specs, out_specs=out_specs, check_vma=False)
```
